32 devices in a mesh: context: 4 (over z), ulysses: 4 (over y, x), dp: 2 (over core).
Axes of the slice: x: 2, y: 2, z: 4, core: 2. Of those that a mesh axis runs over, the one named last changes fastest.
Arguments:
- queries: bfloat16 [4096, 4096], P(('dp', 'context', 'ulysses')), parts along dimension 0, may hold values from -5 to 5
- keys: bfloat16 [4096, 512], P(('dp', 'context', 'ulysses')), parts along dimension 0, may hold values from -5 to 5
- values: bfloat16 [4096, 512], P(('dp', 'context', 'ulysses')), parts along dimension 0, may hold values from -6 to 6
- segments: int32 [4096], P(('dp', 'context')), parts along dimension 0, may hold values from 0 to 7, never falling along the last dimension, each value on 1 to 512 neighbouring positions
- feat_q: bfloat16 [32, 128, 128], P('ulysses'), may hold values from -2 to 2
- feat_k: bfloat16 [4, 128, 128], P('ulysses'), may hold values from -2 to 2
Outputs:
- error: bfloat16 [4096, 4096], P(('dp', 'context'), 'ulysses'), parts along dimension 0
- grad_keys: bfloat16 [4096, 512], P(('dp', 'context'), 'ulysses'), parts along dimension 0
- grad_feat_q: float32 [64, 128, 128], P(('dp', 'ulysses')), parts along dimension 0
- grad_feat_k: float32 [8, 128, 128], P(('dp', 'ulysses')), parts along dimension 0
The draws below stay inside these ranges and needn't reach their ends.
There are 2 independent parts, one for each index of `dp`. The reference program is written for one: setup_inputs(seed, part) draws one part's arguments, and reference() takes and returns one part's arrays. A program takes and returns all parts, laid end to end along the dimension named above; an argument that names none is the same for every part. Nothing has to cross between parts.
Inputs may be any that keep to these rules, and one draw needn't show every extreme that they name: `segments`: document numbers never fall along the sequence; each document covers 1 to 512 positions, and one covers exactly 512.
All inputs are finite; a program needn't handle non-finite values.
Results may differ from the reference program's by a relative error of at most 0.015.
Values may be sent and summed in bfloat16 or wider, within the bound.
No kernel may reach another device: no remote copies, remote signals or barrier semaphores. Data moves between devices by JAX's collectives and lax.ppermute only.
A program may use at most 128 MiB of HBM per device.

```python
import math
import jax
import jax.numpy as jnp
import numpy as np
from jax import lax

H = 32
KVH = 4
E = 128
F = 128
WIN = 128
TOKENS = 2048
DOCS = 8
LONGEST = 512
N_CONTEXT = 4


channel_mean = 0.3


map_offset = 1.2


map_spread = 1.6


def drawn_field(key, salt, width):
    noise = jax.random.normal(jax.random.fold_in(key, salt), (TOKENS, width), jnp.float32)
    return jnp.clip(noise + channel_mean, -5.0, 5.0)


def draw_queries(key, part):
    field = drawn_field(key, 1, H * E)
    return field.astype(jnp.bfloat16)


def draw_keys(key, part):
    field = drawn_field(key, 2, KVH * E)
    return field.astype(jnp.bfloat16)


def draw_values(key, part):
    field = drawn_field(key, 2, KVH * E)
    noise = jax.random.normal(jax.random.fold_in(key, 3), (TOKENS, KVH * E), jnp.float32)
    centred = (field - channel_mean).reshape(TOKENS, KVH, E)
    order = jax.random.permutation(jax.random.fold_in(key, 7), E)
    flips = jnp.where(jax.random.bernoulli(jax.random.fold_in(key, 8), 0.5, (KVH, E)), 1.0, -1.0)
    mixed = 0.7 * flips[None] * centred[:, :, order] + 0.7 * noise.reshape(TOKENS, KVH, E)
    return jnp.clip(mixed.reshape(TOKENS, KVH * E), -6.0, 6.0).astype(jnp.bfloat16)


def map_field(key, salt, heads):
    raw = jax.random.normal(jax.random.fold_in(key, salt), (heads, E, F), jnp.float32)
    return jnp.clip((map_spread * raw - map_offset) / E ** 0.5, -2.0, 2.0)


def draw_feat_q(key, part):
    field = map_field(key, 11, H)
    return field.astype(jnp.bfloat16)


def draw_feat_k(key, part):
    field = map_field(key, 12, KVH)
    return field.astype(jnp.bfloat16)


def length_profile(number_of, total, most, skew):
    weights = [(1 << 20) // math.isqrt(grade ** skew) + 1 for grade in range(2, number_of + 1)]
    surplus, holding = total - most - (number_of - 1), [1] * (number_of - 1)
    while surplus > 0:
        movable = [i for i in range(number_of - 1) if holding[i] < most]
        pool, left = sum([weights[i] for i in movable]), surplus
        for i in movable:
            addition = min(most - holding[i], max(1, left * weights[i] // pool), surplus)
            holding[i] = holding[i] + addition
            surplus = surplus - addition
    return np.array([most] + holding)


def uneven_parts(key, number_of, total, most, skew):
    if number_of == 2:
        one = jax.random.randint(key, (), max(1, total - most), min(most, total - 1) + 1)
        return jnp.stack([one, total - one])
    lengths = jnp.asarray(length_profile(number_of, total, most, skew), jnp.int32)
    couples = (number_of - 1) // 2
    source_of, receiver = lengths[1:1 + 2 * couples:2], lengths[2:2 + 2 * couples:2]
    room = jnp.minimum(source_of - 1, most - receiver)
    passed = jax.random.randint(jax.random.fold_in(key, 1), (couples,), 0, 1 << 20) % (room + 1)
    lengths = lengths.at[1:1 + 2 * couples:2].set(source_of - passed).at[2:2 + 2 * couples:2].set(receiver + passed)
    return lengths[jax.random.permutation(jax.random.fold_in(key, 2), number_of)]


def setup_inputs(seed: int = 0, part: int = 0) -> dict:
    splits = jax.random.split(jax.random.key(seed), 7)
    part_keys = jax.random.split(jax.random.fold_in(splits[6], part), 7)
    queries = draw_queries(jax.random.fold_in(jax.random.fold_in(splits[6], part), 71), part)
    keys = draw_keys(jax.random.fold_in(jax.random.fold_in(splits[6], part), 71), part)
    values = draw_values(jax.random.fold_in(jax.random.fold_in(splits[6], part), 71), part)
    segments = jnp.searchsorted(jnp.cumsum(uneven_parts(part_keys[3], DOCS, TOKENS, LONGEST, 2)), jnp.arange(TOKENS), side="right").astype(jnp.int32)
    feat_q = draw_feat_q(jax.random.fold_in(splits[6], 71), part)
    feat_k = draw_feat_k(jax.random.fold_in(splits[6], 71), part)
    return {"queries": queries, "keys": keys, "values": values, "segments": segments, "feat_q": feat_q, "feat_k": feat_k}


def feature_map(pre):
    return jnp.where(pre > 0, pre + 1.0, jnp.exp(jnp.minimum(pre, 0.0)))

def feature_slope(pre):
    return jnp.where(pre > 0, 1.0, jnp.exp(jnp.minimum(pre, 0.0)))

def join_parts(earlier, later):
    empty_later = later[2] < 0
    keep = (earlier[2] == later[2]) | empty_later
    return (later[0] + jnp.where(keep, earlier[0], 0.0), later[1] + jnp.where(keep, earlier[1], 0.0), jnp.where(empty_later, earlier[2], later[2]))

def mix(form, left, right):
    return jnp.einsum(form, left.astype(jnp.float32), right.astype(jnp.float32), precision=lax.Precision.HIGHEST)

def reference(queries, keys, values, segments, feat_q, feat_k):
    shards = N_CONTEXT
    length = TOKENS // shards
    group = H // KVH
    q_blocks = queries.reshape(shards, length, KVH, group, E)
    k_blocks = keys.reshape(shards, length, KVH, E)
    v_blocks = values.reshape(shards, length, KVH, E)
    s_blocks = segments.reshape(shards, length)
    feat_grouped = feat_q.reshape(KVH, group, E, F)

    def local_state(item):
        key_rows, value_rows, ids = item
        phi_k = feature_map(mix('rge,gef->rgf', key_rows, feat_k)).astype(jnp.bfloat16)
        last_id = ids[length - 1]
        tail = jnp.where((ids == last_id)[:, None, None], phi_k, jnp.zeros_like(phi_k))
        return (mix('rgf,rge->gfe', tail, value_rows), lax.optimization_barrier(jnp.sum(tail.astype(jnp.float32), axis=0)), last_id)
    states, norms, last_ids = lax.map(local_state, (k_blocks, v_blocks, s_blocks))

    def pass_on(carry, item):
        return (join_parts(carry, item), carry)
    anchor = (jnp.zeros((KVH, F, E), jnp.float32), jnp.zeros((KVH, F), jnp.float32), jnp.int32(-1))
    _, (state_in, norm_in, id_in) = lax.scan(pass_on, anchor, (states, norms, last_ids))
    rim_keys = jnp.concatenate([jnp.zeros((1, WIN, KVH, E), keys.dtype), k_blocks[:-1, length - WIN:]], axis=0)
    rim_values = jnp.concatenate([jnp.zeros((1, WIN, KVH, E), values.dtype), v_blocks[:-1, length - WIN:]], axis=0)
    rim_ids = jnp.concatenate([jnp.full((1, WIN), -1, jnp.int32), s_blocks[:-1, length - WIN:].astype(jnp.int32)], axis=0)
    inv_scale = 1.0 / math.sqrt(E)

    def block_pass(item):
        query_rows, key_rows, value_rows, ids, edge_keys, edge_values, edge_ids, c_state, c_norm, c_id = item
        pre_q = mix('rgke,gkef->rgkf', query_rows, feat_grouped)
        phi_q = feature_map(pre_q).astype(jnp.bfloat16)
        phi_k = feature_map(mix('rge,gef->rgf', key_rows, feat_k)).astype(jnp.bfloat16)
        place = jnp.arange(length)
        linked = (place[None, :] <= place[:, None]) & (ids[None, :] == ids[:, None])
        linked = linked[:, None, None, :]
        score = jnp.where(linked, mix('igkf,jgf->igkj', phi_q, phi_k), 0.0)
        take = (ids == c_id)[:, None, None]
        numer = mix('igkj,jge->igke', score.astype(jnp.bfloat16), value_rows) + jnp.where(take[..., None], mix('igkf,gfe->igke', phi_q, c_state), 0.0)
        denom = lax.optimization_barrier(jnp.sum(score, axis=-1)) + jnp.where(take, mix('igkf,gf->igk', phi_q, c_norm), 0.0)
        student = numer / denom[..., None]
        keys_ext = jnp.concatenate([edge_keys, key_rows], axis=0)
        values_ext = jnp.concatenate([edge_values, value_rows], axis=0)
        ids_ext = jnp.concatenate([edge_ids, ids.astype(jnp.int32)], axis=0)
        place_ext = jnp.arange(length + WIN) - WIN
        seen = (place_ext[None, :] <= place[:, None]) & (place_ext[None, :] > place[:, None] - WIN) & (ids_ext[None, :] == ids[:, None])
        logits = jnp.where(seen[:, None, None, :], mix('igke,jge->igkj', query_rows, keys_ext) * inv_scale, -jnp.inf)
        top = lax.optimization_barrier(jnp.max(logits, axis=-1, keepdims=True))
        probs = jnp.exp(logits - top)
        teacher = mix('igkj,jge->igke', probs.astype(jnp.bfloat16), values_ext) / lax.optimization_barrier(jnp.sum(probs, axis=-1))[..., None]
        gap = student - teacher
        upstream = 32.0 * gap
        d_numer = (upstream / denom[..., None]).astype(jnp.bfloat16)
        d_denom = -lax.optimization_barrier(jnp.sum(upstream * student, axis=-1)) / denom
        d_score = jnp.where(linked, mix('igke,jge->igkj', d_numer, value_rows) + d_denom[..., None], 0.0).astype(jnp.bfloat16)
        d_phi_q = mix('igkj,jgf->igkf', d_score, phi_k) + jnp.where(take[..., None], mix('gfe,igke->igkf', c_state, d_numer) + d_denom[..., None] * c_norm[None, :, None, :], 0.0)
        d_phi_k = mix('igkj,igkf->jgf', d_score, phi_q)
        head_rows = (ids == ids[0])[:, None, None, None]
        phi_head = jnp.where(head_rows, phi_q, jnp.zeros_like(phi_q))
        cot_state = mix('igkf,igke->gfe', phi_head, d_numer)
        cot_norm = lax.optimization_barrier(jnp.sum(jnp.where(head_rows, d_denom[..., None] * phi_q.astype(jnp.float32), 0.0), axis=(0, 2)))
        d_pre_q = (d_phi_q * feature_slope(pre_q)).astype(jnp.bfloat16)
        grad_q = mix('rgke,rgkf->gkef', query_rows, d_pre_q)
        return (gap.astype(jnp.bfloat16), d_phi_k, cot_state, cot_norm, ids[0], grad_q)
    gaps, d_phi_ks, cot_states, cot_norms, first_ids, grad_qs = lax.map(block_pass, (q_blocks, k_blocks, v_blocks, s_blocks, rim_keys, rim_values, rim_ids, state_in, norm_in, id_in))
    _, (back_state, back_norm, back_id) = lax.scan(pass_on, anchor, (cot_states, cot_norms, first_ids), reverse=True)

    def finish(item):
        key_rows, value_rows, ids, d_phi_k, b_state, b_norm, b_id = item
        pre_k = mix('rge,gef->rgf', key_rows, feat_k)
        take = (ids == b_id)[:, None, None]
        d_phi_k = d_phi_k + jnp.where(take, mix('gfe,jge->jgf', b_state, value_rows) + b_norm[None], 0.0)
        d_pre_k = (d_phi_k * feature_slope(pre_k)).astype(jnp.bfloat16)
        key_grad = mix('jgf,gef->jge', d_pre_k, feat_k).astype(jnp.bfloat16)
        return (key_grad, mix('rge,rgf->gef', key_rows, d_pre_k))
    key_grads, grad_ks = lax.map(finish, (k_blocks, v_blocks, s_blocks, d_phi_ks, back_state, back_norm, back_id))
    scale = 1.0 / math.sqrt(TOKENS)
    error = gaps.reshape(TOKENS, H * E)
    grad_keys = key_grads.reshape(TOKENS, KVH * E)
    grad_feat_q = lax.optimization_barrier(jnp.sum(grad_qs, axis=0)).reshape(H, E, F) * scale
    grad_feat_k = lax.optimization_barrier(jnp.sum(grad_ks, axis=0)) * scale
    return (error, grad_keys, grad_feat_q, grad_feat_k)
```

```python
import functools
import math

import jax
import jax.numpy as jnp
from jax import lax
from jax.experimental import pallas as pl
from jax.experimental.pallas import tpu as pltpu
from jax.sharding import PartitionSpec as P

WIN = 128
T = 128
SPLITS = 2
BF = jnp.bfloat16
F32 = jnp.float32


def dot(left, right):
    return lax.dot_general(left, right, (((1,), (0,)), ((), ())), preferred_element_type=F32)


def dot_nt(left, right):
    return lax.dot_general(left, right, (((1,), (1,)), ((), ())), preferred_element_type=F32)


def dot_tn(left, right):
    return lax.dot_general(left, right, (((0,), (0,)), ((), ())), preferred_element_type=F32)


def halves(whole):
    upper = whole.astype(BF)
    return upper, (whole - upper.astype(F32)).astype(BF)


def feature(pre):
    slope = jnp.exp(jnp.minimum(pre, 0.0))
    return slope + jnp.maximum(pre, 0.0), slope


def as_columns(row):
    return jnp.broadcast_to(row, (T, T)).T


def marker(rows):
    lane = lax.broadcasted_iota(jnp.int32, (rows, T), 1)
    return jnp.where((lane == 0) | (lane == T // 2), 1.0, 0.0).astype(BF)


def place_rows(target, pieces, axis):
    here = lax.axis_index(axis)
    for step, piece in enumerate(pieces):
        start = pl.multiple_of((here ^ step) * T, T)
        target[pl.ds(start, T), :] = piece[...]


def attend(*refs, tiles, heads, first, last, extra, scale, inv):
    refs = list(refs)

    def take(count):
        taken = refs[:count]
        del refs[:count]
        return taken

    kv_in, past_in, q_in = take(tiles), take(tiles), take(tiles)
    seg_ref, past_seg_ref, seg_scalar, fq_ref, fk_ref = take(5)
    extra_ref = take(1)[0] if extra else None
    if not first:
        _, dpk_in, cot_in = take(3)
    err_ref, gq_ref = take(2)
    if last:
        gk_ref, msg_ref, gkeys_ref, val_ref, slope_out = take(5)
    else:
        dpk_out, cot_out = take(2)
    kv, past, qs, phis, slopes, dpres = refs
    place_rows(kv, kv_in, "ulysses")
    place_rows(past, past_in, "ulysses")
    place_rows(qs, q_in, "ulysses")
    length = tiles * T
    group = heads * T

    k_rows, v_rows = kv[:, :T], kv[:, T:]
    kp_rows, vp_rows = past[:, :T], past[:, T:]
    fk = fk_ref[0]
    phi_k, slope_k = feature(dot(k_rows, fk))
    phi_k = phi_k.astype(BF)
    phi_kp, slope_kp = feature(dot(kp_rows, fk))
    first_id = seg_scalar[0, 0].astype(F32)
    seg = seg_ref[...].astype(F32)
    past_seg = past_seg_ref[...].astype(F32)
    seg_cols = [as_columns(seg[i : i + 1]) for i in range(tiles)]
    past_cols = [as_columns(past_seg[i : i + 1]) for i in range(tiles)]
    past_take = jnp.concatenate([c == first_id for c in past_cols], axis=0)
    phi_kp = jnp.where(past_take, phi_kp, 0.0).astype(BF)
    ones = jnp.ones((length, T), BF)
    mark = marker(length)
    v_one = jnp.concatenate([v_rows, ones], axis=1)
    v_mark = jnp.concatenate([v_rows, mark], axis=1)
    vp_one = jnp.concatenate([vp_rows, ones], axis=1)
    state = dot_tn(phi_kp, vp_one)
    if extra:
        state = state + extra_ref[...]
    st_hi, st_lo = halves(state)
    state_mark = jnp.concatenate([jnp.ones((T, T), BF), marker(T)], axis=1)
    sw_hi, sw_lo = st_hi * state_mark, st_lo * state_mark

    for h in range(heads):
        phi, slope = feature(dot(qs[:, h * T : (h + 1) * T], fq_ref[h]))
        phi = phi.astype(BF)
        for i in range(tiles):
            phis[i, h * T : (h + 1) * T, :] = phi[i * T : (i + 1) * T]
            slopes[i, h * T : (h + 1) * T, :] = slope[i * T : (i + 1) * T]

    t_pos = lax.broadcasted_iota(jnp.int32, (T, T), 0)
    s_pos = lax.broadcasted_iota(jnp.int32, (T, T), 1)
    half_lane = lax.broadcasted_iota(jnp.int32, (group, T), 1) < T // 2
    dpk = [jnp.zeros((T, T), F32)] * tiles
    cot = jnp.zeros((T, 2 * T), F32)
    if not first:
        dpk = [dpk_in[:, j * T : (j + 1) * T] for j in range(tiles)]
        cot = cot_in[...]

    def stack(tile):
        return jnp.concatenate([tile] * heads, axis=0)

    for i in range(tiles):
        n = (i + 1) * T
        phi = phis[i]
        same = [seg_cols[i] == seg[j : j + 1] for j in range(i + 1)]
        same[i] = same[i] & (s_pos <= t_pos)
        linked = stack(jnp.concatenate([m.astype(F32).astype(BF) for m in same], axis=1))
        lead = (seg_cols[i] == first_id).astype(F32).astype(BF)
        lead = stack(jnp.concatenate([lead, lead], axis=1))
        scores = dot_nt(phi, phi_k[:n]).astype(BF) * linked
        phi_lead = phi * lead[:, :T]
        both = dot(scores, v_one[:n]) + dot(phi_lead, st_hi) + dot(phi_lead, st_lo)
        inv_denom = 1.0 / both[:, T:]
        student = both[:, :T] * inv_denom

        if i == 0:
            rim_k, rim_v, rim_seg = kp_rows[-T:], vp_one[-T:], past_seg[tiles - 1 : tiles]
        else:
            rim_k, rim_v, rim_seg = k_rows[n - 2 * T : n - T], v_one[n - 2 * T : n - T], seg[i - 1 : i]
        seen = (seg_cols[i] == rim_seg) & (s_pos > t_pos)
        off = jnp.concatenate([jnp.where(m, 0.0, -1e30) for m in (seen, same[i])], axis=1)
        q_rows = jnp.concatenate([qs[n - T : n, h * T : (h + 1) * T] for h in range(heads)], axis=0)
        logits = dot_nt(q_rows, jnp.concatenate([rim_k, k_rows[n - T : n]], axis=0)) + stack(off)
        top = jnp.max(logits, axis=-1, keepdims=True)
        probs = jnp.exp((logits - top) * inv).astype(BF)
        soft = dot(probs, jnp.concatenate([rim_v, v_one[n - T : n]], axis=0))
        gap = student - soft[:, :T] / soft[:, T:]
        for h in range(heads):
            err_ref[n - T : n, h * T : (h + 1) * T] = gap[h * T : (h + 1) * T].astype(BF)

        up = (32.0 * gap) * inv_denom
        d_denom = -jnp.sum(up * student, axis=-1, keepdims=True)
        d_hi, d_lo = halves(jnp.broadcast_to(d_denom, (group, T)))
        tail = jnp.where(half_lane, d_hi.astype(F32), d_lo.astype(F32)).astype(BF)
        d_both = jnp.concatenate([up.astype(BF), tail], axis=1)
        d_scores = dot_nt(d_both, v_mark[:n]).astype(BF) * linked
        d_lead = d_both * lead
        d_phi = dot(d_scores, phi_k[:n]) + dot_nt(d_lead, sw_hi) + dot_nt(d_lead, sw_lo)
        dpres[i] = (d_phi * slopes[i]).astype(BF)
        phi_t = phi.T
        back = dot(phi_t, d_scores)
        for j in range(i + 1):
            dpk[j] = dpk[j] + back[:, j * T : (j + 1) * T]
        cot = cot + dot(phi_t, d_lead)

    for h in range(heads):
        d_pre = jnp.concatenate([dpres[i, h * T : (h + 1) * T, :] for i in range(tiles)], axis=0)
        gq_ref[h] = (dot_tn(qs[:, h * T : (h + 1) * T], d_pre) * scale).astype(BF)

    if not last:
        for j in range(tiles):
            dpk_out[:, j * T : (j + 1) * T] = dpk[j]
        cot_out[...] = cot
        return
    d_phi_k = jnp.concatenate([part.T for part in dpk], axis=0)
    d_pre_k = (d_phi_k * slope_k).astype(BF)
    cot_hi, cot_lo = halves(cot)
    vp_mark = jnp.concatenate([vp_rows, mark], axis=1)
    cross = dot_nt(vp_mark, cot_hi) + dot_nt(vp_mark, cot_lo)
    cross = jnp.where(past_take, cross * slope_kp, 0.0).astype(BF)
    gk_ref[0] = ((dot_tn(k_rows, d_pre_k) + dot_tn(kp_rows, cross)) * scale).astype(BF)
    msg_ref[...] = cot_hi
    gkeys_ref[...] = dot_nt(d_pre_k, fk)
    val_ref[...] = v_rows
    slope_out[...] = slope_k


def settle(seg_ref, next_seg, msg_ref, gkeys_ref, val_ref, slope_ref, fk_ref, out_ref, *, tiles):
    next_id = next_seg[0, 0].astype(F32)
    seg = seg_ref[...].astype(F32)
    linked = jnp.concatenate([as_columns(seg[i : i + 1]) == next_id for i in range(tiles)], axis=0)
    v_mark = jnp.concatenate([val_ref[...], marker(tiles * T)], axis=1)
    back = jnp.where(linked, dot_nt(v_mark, msg_ref[...]) * slope_ref[...], 0.0).astype(BF)
    out_ref[...] = (gkeys_ref[...] + dot_nt(back, fk_ref[0])).astype(BF)


def merge(*refs, count):
    *pieces, out_ref = refs
    here = lax.axis_index("context")
    rows = pieces[0].shape[0]
    for step, piece in enumerate(pieces):
        start = pl.multiple_of((here ^ step) * rows, rows)
        out_ref[pl.ds(start, rows), :] = piece[...].astype(F32)


VMEM = pl.BlockSpec(memory_space=pltpu.VMEM)
SMEM = pl.BlockSpec(memory_space=pltpu.SMEM)
ANY = pl.BlockSpec(memory_space=pl.ANY)
PARAMS = dict(vmem_limit_bytes=48 * 1024 * 1024)


def swap(block, axis, step):
    return lax.ppermute(block, axis, [(i, i ^ step) for i in range(lax.axis_size(axis))])


def shift(block, axis, distance):
    devices = range(lax.axis_size(axis))
    return lax.ppermute(block, axis, [(i - distance, i) for i in devices if i - distance in devices])


def sum_over_context(part):
    count, here = lax.axis_size("context"), lax.axis_index("context")
    rows = part.shape[0] // count
    got = []
    for step in range(count):
        piece = lax.dynamic_slice_in_dim(part, (here ^ step) * rows, rows, 0)
        got.append(piece if step == 0 else swap(piece, "context", step))
    total = functools.reduce(jnp.add, [g.astype(F32) for g in got]).astype(BF)
    pieces = [total] + [swap(total, "context", step) for step in range(1, count)]
    return pl.pallas_call(
        functools.partial(merge, count=count),
        out_shape=jax.ShapeDtypeStruct(part.shape, F32),
        in_specs=[VMEM] * count,
        out_specs=VMEM,
    )(*pieces)


def on_device(queries, keys, values, segments, feat_q, feat_k):
    tiles, here = lax.axis_size("ulysses"), lax.axis_index("ulysses")
    heads, width, _ = feat_q.shape
    length = segments.shape[0]
    part = heads // SPLITS
    kv_own = [
        jnp.concatenate(
            [lax.dynamic_slice_in_dim(a, (here ^ step) * width, width, 1) for a in (keys, values)],
            axis=1,
        )
        for step in range(tiles)
    ]
    kv = [kv_own[0]] + [swap(kv_own[step], "ulysses", step) for step in range(1, tiles)]
    past = [shift(piece, "context", 1) for piece in kv]
    q = []
    for p in range(SPLITS):
        cut = [
            lax.dynamic_slice_in_dim(
                queries, ((here ^ step) * heads + p * part) * width, part * width, 1
            )
            for step in range(tiles)
        ]
        q.append([cut[0]] + [swap(cut[step], "ulysses", step) for step in range(1, tiles)])
    seg = segments.reshape(tiles, T)
    past_seg = jnp.where(lax.axis_index("context") > 0, shift(seg, "context", 1), -1)
    next_seg = shift(seg, "context", -1)

    scale = 1.0 / math.sqrt(length * lax.axis_size("context"))
    inv = 1.0 / math.sqrt(width)
    carry = []
    grads = []
    for p in range(SPLITS):
        first, last = p == 0, p == SPLITS - 1
        in_specs = [VMEM] * (3 * tiles + 2) + [SMEM]
        in_specs += [pl.BlockSpec((part, width, width), functools.partial(lambda p, _: (p, 0, 0), p))]
        in_specs += [VMEM]
        args = [*kv, *past, *q[p], seg, past_seg, seg, feat_q, feat_k]
        aliases = {}
        if not first:
            aliases = {len(args): 0}
            args += carry
            in_specs += [ANY, VMEM, VMEM]
        out_shape = [
            jax.ShapeDtypeStruct((length, heads * width), BF),
            jax.ShapeDtypeStruct((part, width, width), BF),
        ]
        out_specs = [
            pl.BlockSpec((length, part * width), functools.partial(lambda p, _: (0, p), p)),
            VMEM,
        ]
        if last:
            out_shape += [
                jax.ShapeDtypeStruct((1, width, width), BF),
                jax.ShapeDtypeStruct((width, 2 * width), BF),
                jax.ShapeDtypeStruct((length, width), F32),
                jax.ShapeDtypeStruct((length, width), BF),
                jax.ShapeDtypeStruct((length, width), F32),
            ]
            out_specs += [VMEM] * 5
        else:
            out_shape += [
                jax.ShapeDtypeStruct((width, length), F32),
                jax.ShapeDtypeStruct((width, 2 * width), F32),
            ]
            out_specs += [VMEM] * 2
        outs = pl.pallas_call(
            functools.partial(
                attend,
                tiles=tiles,
                heads=part,
                first=first,
                last=last,
                extra=False,
                scale=scale,
                inv=inv,
            ),
            grid=(1,),
            out_shape=out_shape,
            in_specs=in_specs,
            out_specs=out_specs,
            scratch_shapes=[
                pltpu.VMEM((length, 2 * width), BF),
                pltpu.VMEM((length, 2 * width), BF),
                pltpu.VMEM((length, part * width), BF),
                pltpu.VMEM((tiles, part * T, width), BF),
                pltpu.VMEM((tiles, part * T, width), F32),
                pltpu.VMEM((tiles, part * T, width), BF),
            ],
            input_output_aliases=aliases,
            compiler_params=pltpu.CompilerParams(**PARAMS),
            cost_estimate=pl.CostEstimate(
                flops=part * 500_000_000, bytes_accessed=4_000_000, transcendentals=0
            ),
        )(*args)
        grads.append(outs[1])
        carry = [outs[0], outs[2], outs[3]]
    error, _, grad_k, msg, gkeys, v_rows, slope_k = outs
    msg = shift(msg, "context", -1)
    grad_keys = pl.pallas_call(
        functools.partial(settle, tiles=tiles),
        out_shape=jax.ShapeDtypeStruct((length, width), BF),
        in_specs=[VMEM, SMEM, VMEM, VMEM, VMEM, VMEM, VMEM],
        out_specs=VMEM,
    )(seg, next_seg, msg, gkeys, v_rows, slope_k, feat_k)
    sums = []
    for p, grad in enumerate(grads):
        block = grad.reshape(part * width, width)
        if p == SPLITS - 1:
            block = jnp.concatenate([block, grad_k[0]], axis=0)
        sums.append(sum_over_context(block))
    grad_feat_k = sums[-1][part * width :].reshape(1, width, width)
    sums[-1] = sums[-1][: part * width]
    grad_feat_q = jnp.concatenate(sums, axis=0).reshape(heads, width, width)
    return error, grad_keys, grad_feat_q, grad_feat_k


def solution(mesh):
    in_specs = (
        P(("dp", "context", "ulysses"), None),
        P(("dp", "context", "ulysses"), None),
        P(("dp", "context", "ulysses"), None),
        P(("dp", "context")),
        P("ulysses", None, None),
        P("ulysses", None, None),
    )
    out_specs = (
        P(("dp", "context"), "ulysses"),
        P(("dp", "context"), "ulysses"),
        P(("dp", "ulysses"), None, None),
        P(("dp", "ulysses"), None, None),
    )
    return jax.shard_map(
        on_device, mesh=mesh, in_specs=in_specs, out_specs=out_specs, check_vma=False
    )
```

```python
import functools
import math

import jax
import jax.numpy as jnp
from jax import lax
from jax.experimental import pallas as pl
from jax.experimental.pallas import tpu as pltpu
from jax.sharding import PartitionSpec as P

T = 128
BF = jnp.bfloat16
F32 = jnp.float32


def dot(left, right):
    return lax.dot_general(left, right, (((1,), (0,)), ((), ())), preferred_element_type=F32)


def dot_nt(left, right):
    return lax.dot_general(left, right, (((1,), (1,)), ((), ())), preferred_element_type=F32)


def dot_tn(left, right):
    return lax.dot_general(left, right, (((0,), (0,)), ((), ())), preferred_element_type=F32)


def halves(whole):
    upper = whole.astype(BF)
    return upper, (whole - upper.astype(F32)).astype(BF)


def feature(pre):
    slope = jnp.exp(jnp.minimum(pre, 0.0))
    return slope + jnp.maximum(pre, 0.0), slope


def as_columns(row):
    return jnp.broadcast_to(row, (T, T)).T


def marker(rows):
    lane = lax.broadcasted_iota(jnp.int32, (rows, T), 1)
    return jnp.where((lane == 0) | (lane == T // 2), 1.0, 0.0).astype(BF)


def place_rows(target, pieces, axis):
    here = lax.axis_index(axis) if len(pieces) > 1 else jnp.int32(0)
    rows = pieces[0].shape[0]
    for step, piece in enumerate(pieces):
        start = pl.multiple_of((here ^ step) * rows, 16)
        target[pl.ds(start, rows), :] = piece[...].astype(target.dtype)


def attend(*refs, tiles, heads, shares, extra, scale, inv):
    refs = list(refs)

    def take(count):
        taken = refs[:count]
        del refs[:count]
        return taken

    kv_in, q_in = take(tiles), take(tiles)
    past_in, seg_ref, past_seg_ref, seg_scalar, fq_ref, fk_ref = take(6)
    extra_ref = take(1)[0] if extra else None
    err_ref, msg_ref, gkeys_ref, kv, slope_out = take(5)
    share_refs = take(shares)
    past, qs, phis, slopes, dpres, grads = refs
    place_rows(kv, kv_in, "ulysses")
    place_rows(past, [past_in.at[d * T : (d + 1) * T] for d in range(tiles)], "ulysses")
    place_rows(qs, q_in, "ulysses")
    length = tiles * T
    group = heads * T

    k_rows, v_rows = kv[:, :T], kv[:, T:]
    kp_rows, vp_rows = past[:, :T], past[:, T:]
    fk = fk_ref[0]
    phi_k, slope_k = feature(dot(k_rows, fk))
    phi_k = phi_k.astype(BF)
    phi_kp, slope_kp = feature(dot(kp_rows, fk))
    first_id = seg_scalar[0, 0].astype(F32)
    seg = seg_ref[...].astype(F32)
    past_seg = past_seg_ref[...].astype(F32)
    past_seg = jnp.where(lax.axis_index("context") > 0, past_seg, -1.0)
    seg_cols = [as_columns(seg[i : i + 1]) for i in range(tiles)]
    past_cols = [as_columns(past_seg[i : i + 1]) for i in range(tiles)]
    past_take = jnp.concatenate([c == first_id for c in past_cols], axis=0)
    phi_kp = jnp.where(past_take, phi_kp, 0.0).astype(BF)
    ones = jnp.ones((length, T), BF)
    mark = marker(length)
    v_one = jnp.concatenate([v_rows, ones], axis=1)
    v_mark = jnp.concatenate([v_rows, mark], axis=1)
    vp_one = jnp.concatenate([vp_rows, ones], axis=1)
    state = dot_tn(phi_kp, vp_one)
    if extra:
        state = state + extra_ref[...]
    st_hi, st_lo = halves(state)
    state_mark = jnp.concatenate([jnp.ones((T, T), BF), marker(T)], axis=1)
    sw_hi, sw_lo = st_hi * state_mark, st_lo * state_mark

    for h in range(heads):
        phi, slope = feature(dot(qs[:, h * T : (h + 1) * T], fq_ref[h]))
        phi = phi.astype(BF)
        for i in range(tiles):
            phis[i, h * T : (h + 1) * T, :] = phi[i * T : (i + 1) * T]
            slopes[i, h * T : (h + 1) * T, :] = slope[i * T : (i + 1) * T]

    t_pos = lax.broadcasted_iota(jnp.int32, (T, T), 0)
    s_pos = lax.broadcasted_iota(jnp.int32, (T, T), 1)
    half_lane = lax.broadcasted_iota(jnp.int32, (group, T), 1) < T // 2
    dpk = [jnp.zeros((T, T), F32)] * tiles
    cot = jnp.zeros((T, 2 * T), F32)

    def stack(tile):
        return jnp.concatenate([tile] * heads, axis=0)

    for i in range(tiles):
        n = (i + 1) * T
        phi = phis[i]
        same = [seg_cols[i] == seg[j : j + 1] for j in range(i + 1)]
        same[i] = same[i] & (s_pos <= t_pos)
        linked = stack(jnp.concatenate([m.astype(F32).astype(BF) for m in same], axis=1))
        lead = (seg_cols[i] == first_id).astype(F32).astype(BF)
        lead = stack(jnp.concatenate([lead, lead], axis=1))
        scores = dot_nt(phi, phi_k[:n]).astype(BF) * linked
        phi_lead = phi * lead[:, :T]
        both = dot(scores, v_one[:n]) + dot(phi_lead, st_hi) + dot(phi_lead, st_lo)
        inv_denom = 1.0 / both[:, T:]
        student = both[:, :T] * inv_denom

        if i == 0:
            rim_k, rim_v, rim_seg = kp_rows[-T:], vp_one[-T:], past_seg[tiles - 1 : tiles]
        else:
            rim_k, rim_v, rim_seg = k_rows[n - 2 * T : n - T], v_one[n - 2 * T : n - T], seg[i - 1 : i]
        seen = (seg_cols[i] == rim_seg) & (s_pos > t_pos)
        off = jnp.concatenate([jnp.where(m, 0.0, -1e30) for m in (seen, same[i])], axis=1)
        q_rows = jnp.concatenate([qs[n - T : n, h * T : (h + 1) * T] for h in range(heads)], axis=0)
        logits = dot_nt(q_rows, jnp.concatenate([rim_k, k_rows[n - T : n]], axis=0)) + stack(off)
        top = jnp.max(logits, axis=-1, keepdims=True)
        probs = jnp.exp((logits - top) * inv).astype(BF)
        soft = dot(probs, jnp.concatenate([rim_v, v_one[n - T : n]], axis=0))
        gap = student - soft[:, :T] / soft[:, T:]
        for h in range(heads):
            err_ref[n - T : n, h * T : (h + 1) * T] = gap[h * T : (h + 1) * T].astype(BF)

        up = (32.0 * gap) * inv_denom
        d_denom = -jnp.sum(up * student, axis=-1, keepdims=True)
        d_hi, d_lo = halves(jnp.broadcast_to(d_denom, (group, T)))
        tail = jnp.where(half_lane, d_hi.astype(F32), d_lo.astype(F32)).astype(BF)
        d_both = jnp.concatenate([up.astype(BF), tail], axis=1)
        d_scores = dot_nt(d_both, v_mark[:n]).astype(BF) * linked
        d_lead = d_both * lead
        d_phi = dot(d_scores, phi_k[:n]) + dot_nt(d_lead, sw_hi) + dot_nt(d_lead, sw_lo)
        dpres[i] = (d_phi * slopes[i]).astype(BF)
        phi_t = phi.T
        back = dot(phi_t, d_scores)
        for j in range(i + 1):
            dpk[j] = dpk[j] + back[:, j * T : (j + 1) * T]
        cot = cot + dot(phi_t, d_lead)

    for h in range(heads):
        d_pre = jnp.concatenate([dpres[i, h * T : (h + 1) * T, :] for i in range(tiles)], axis=0)
        grad = dot_tn(qs[:, h * T : (h + 1) * T], d_pre)
        grads[h * T : (h + 1) * T, :] = (grad * scale).astype(BF)

    d_phi_k = jnp.concatenate([part.T for part in dpk], axis=0)
    d_pre_k = (d_phi_k * slope_k).astype(BF)
    cot_hi, cot_lo = halves(cot)
    vp_mark = jnp.concatenate([vp_rows, mark], axis=1)
    cross = dot_nt(vp_mark, cot_hi) + dot_nt(vp_mark, cot_lo)
    cross = jnp.where(past_take, cross * slope_kp, 0.0).astype(BF)
    grad = dot_tn(k_rows, d_pre_k) + dot_tn(kp_rows, cross)
    grads[group : group + T, :] = (grad * scale).astype(BF)
    msg_lane = lax.broadcasted_iota(jnp.int32, (T, 2 * T), 1)
    msg_ref[...] = jnp.where(msg_lane == T + 1, first_id, cot_hi.astype(F32)).astype(BF)
    gkeys_ref[...] = dot_nt(d_pre_k, fk)
    slope_out[...] = slope_k
    rows = (heads + 1) * T // shares
    here = lax.axis_index("context") if shares > 1 else jnp.int32(0)
    for step, share in enumerate(share_refs):
        share[...] = grads[pl.ds(pl.multiple_of((here ^ step) * rows, 16), rows), :]


def settle(seg_ref, msg_ref, gkeys_ref, kv_ref, slope_ref, fk_ref, out_ref, *, tiles):
    ids = msg_ref[:16, T:].astype(F32)
    next_id = jnp.max(jnp.where(lax.broadcasted_iota(jnp.int32, ids.shape, 1) == 1, ids, -1.0))
    seg = seg_ref[...].astype(F32)
    linked = jnp.concatenate([as_columns(seg[i : i + 1]) == next_id for i in range(tiles)], axis=0)
    v_mark = jnp.concatenate([kv_ref[:, T:], marker(tiles * T)], axis=1)
    back = jnp.where(linked, dot_nt(v_mark, msg_ref[...]) * slope_ref[...], 0.0).astype(BF)
    out_ref[...] = (gkeys_ref[...] + dot_nt(back, fk_ref[0])).astype(BF)


def add_up(*refs):
    *pieces, out_ref = refs
    out_ref[...] = functools.reduce(jnp.add, [p[...].astype(F32) for p in pieces]).astype(BF)


def merge(*refs):
    *pieces, q_ref, k_ref, whole = refs
    place_rows(whole, pieces, "context")
    rows = q_ref.shape[0]
    q_ref[...] = whole[:rows]
    k_ref[...] = whole[rows:]


VMEM = pl.BlockSpec(memory_space=pltpu.VMEM)
SMEM = pl.BlockSpec(memory_space=pltpu.SMEM)


def call(kernel, out_shape, in_specs, args, scratch=(), flops=0, moved=0, **options):
    return pl.pallas_call(
        functools.partial(kernel, **options),
        grid=(1,),
        out_shape=out_shape,
        in_specs=in_specs,
        out_specs=jax.tree.map(lambda _: VMEM, out_shape),
        scratch_shapes=scratch,
        compiler_params=pltpu.CompilerParams(vmem_limit_bytes=48 * 1024 * 1024),
        cost_estimate=pl.CostEstimate(flops=flops, bytes_accessed=moved, transcendentals=0),
    )(*args)


def swap(block, axis, step):
    return lax.ppermute(block, axis, [(i, i ^ step) for i in range(lax.axis_size(axis))])


def shift(block, axis, distance):
    devices = range(lax.axis_size(axis))
    return lax.ppermute(block, axis, [(i - distance, i) for i in devices if i - distance in devices])


def far_state(packed, seg, feat_k):
    count, here = lax.axis_size("context"), lax.axis_index("context")
    tiles, spot = lax.axis_size("ulysses"), lax.axis_index("ulysses")
    ids = jnp.take(seg, spot ^ jnp.arange(tiles), axis=0).reshape(-1)
    first_id, last_id = seg[0, 0], seg[-1, -1]
    phi = feature(dot(packed[:, :T], feat_k[0]))[0].astype(BF)
    phi = jnp.where((ids == last_id)[:, None], phi, jnp.zeros_like(phi))
    local = dot_tn(phi, jnp.concatenate([packed[:, T:], jnp.ones_like(phi)], axis=1))
    states, last_ids = lax.all_gather((local, last_id), "context")
    keep = (last_ids == first_id) & (jnp.arange(count) < here - 1)
    return jnp.sum(jnp.where(keep[:, None, None], states, 0.0), axis=0)


def far_cotangent(cot, kv, slope, seg):
    count, here = lax.axis_size("context"), lax.axis_index("context")
    ids = seg.reshape(-1)
    cot = cot.astype(F32) * jnp.concatenate([jnp.ones((T, T)), marker(T)], axis=1)
    cots, first_ids = lax.all_gather((cot, ids[0]), "context")
    keep = (first_ids == ids[-1]) & (jnp.arange(count) > here + 1)
    total = jnp.sum(jnp.where(keep[:, None, None], cots, 0.0), axis=0)
    v_mark = jnp.concatenate([kv[:, T:], marker(ids.shape[0])], axis=1)
    back = jnp.where((ids == ids[-1])[:, None], dot_nt(v_mark, total.astype(BF)) * slope, 0.0)
    return total, dot_tn(kv[:, :T], back.astype(BF))


def on_device(queries, keys, values, segments, feat_q, feat_k):
    tiles, here = lax.axis_size("ulysses"), lax.axis_index("ulysses")
    count = lax.axis_size("context")
    heads, width, _ = feat_q.shape
    length = segments.shape[0]
    far = count * length // 4 > length
    rows = (heads + 1) * width
    shares = count if count <= 4 and rows % (16 * count) == 0 else 1
    scale = 1.0 / math.sqrt(length * count)
    inv = 1.0 / math.sqrt(width)

    kv = [
        jnp.concatenate(
            [lax.dynamic_slice_in_dim(a, (here ^ step) * width, width, 1) for a in (keys, values)],
            axis=1,
        )
        for step in range(tiles)
    ]
    q = [
        lax.dynamic_slice_in_dim(queries, (here ^ step) * heads * width, heads * width, 1)
        for step in range(tiles)
    ]
    kv, q = lax.optimization_barrier((kv, q))
    kv = kv[:1] + [swap(kv[step], "ulysses", step) for step in range(1, tiles)]
    q = q[:1] + [swap(q[step], "ulysses", step) for step in range(1, tiles)]
    seg = segments.reshape(tiles, T)
    packed = jnp.concatenate(kv, axis=0)
    past = shift(packed, "context", 1)
    past_seg = shift(seg, "context", 1)

    args = [*kv, *q, past, seg, past_seg, seg, feat_q, feat_k]
    in_specs = [VMEM] * (2 * tiles + 3) + [SMEM, VMEM, VMEM]
    if far:
        args.append(far_state(packed[:length], seg, feat_k))
        in_specs.append(VMEM)
    error, msg, gkeys, kv_rows, slope_k, *grads = call(
        attend,
        [
            jax.ShapeDtypeStruct((length, heads * width), BF),
            jax.ShapeDtypeStruct((width, 2 * width), BF),
            jax.ShapeDtypeStruct((length, width), F32),
            jax.ShapeDtypeStruct((length, 2 * width), BF),
            jax.ShapeDtypeStruct((length, width), F32),
        ]
        + [jax.ShapeDtypeStruct((rows // shares, width), BF)] * shares,
        in_specs,
        args,
        [
            pltpu.VMEM((length, 2 * width), BF),
            pltpu.VMEM((length, heads * width), BF),
            pltpu.VMEM((tiles, heads * T, width), BF),
            pltpu.VMEM((tiles, heads * T, width), F32),
            pltpu.VMEM((tiles, heads * T, width), BF),
            pltpu.VMEM((rows, width), BF),
        ],
        flops=4_000_000_000,
        moved=4_000_000,
        tiles=tiles,
        heads=heads,
        shares=shares,
        extra=far,
        scale=scale,
        inv=inv,
    )
    came = shift(msg, "context", -1)
    if far:
        more, grad_more = far_cotangent(msg, kv_rows, slope_k, seg)
        came = (came.astype(F32) + more).astype(BF)
        grad_more = (grad_more * scale).astype(BF)
        grads = [grads[0].at[heads * width :].add(grad_more)]
    if shares > 1:
        got = grads[:1] + [swap(grads[step], "context", step) for step in range(shares - 1, 0, -1)]
        came, *got = lax.optimization_barrier((came, *got))
        total = call(
            add_up, jax.ShapeDtypeStruct((rows // shares, width), BF), [VMEM] * shares, got
        )
        pieces = [swap(total, "context", step) for step in range(shares - 1, 0, -1)]
        pieces = [total] + pieces[::-1]
    else:
        pieces = [lax.psum(grads[0], "context")]
    grad_keys = call(
        settle,
        jax.ShapeDtypeStruct((length, width), BF),
        [VMEM] * 6,
        [seg, came, gkeys, kv_rows, slope_k, feat_k],
        tiles=tiles,
    )
    grad_q, grad_k = call(
        merge,
        [
            jax.ShapeDtypeStruct((heads * width, width), F32),
            jax.ShapeDtypeStruct((width, width), F32),
        ],
        [VMEM] * shares,
        pieces,
        [pltpu.VMEM((rows, width), F32)],
    )
    return (
        error,
        grad_keys,
        grad_q.reshape(heads, width, width),
        grad_k.reshape(1, width, width),
    )


def solution(mesh):
    in_specs = (
        P(("dp", "context", "ulysses"), None),
        P(("dp", "context", "ulysses"), None),
        P(("dp", "context", "ulysses"), None),
        P(("dp", "context")),
        P("ulysses", None, None),
        P("ulysses", None, None),
    )
    out_specs = (
        P(("dp", "context"), "ulysses"),
        P(("dp", "context"), "ulysses"),
        P(("dp", "ulysses"), None, None),
        P(("dp", "ulysses"), None, None),
    )
    return jax.shard_map(
        on_device, mesh=mesh, in_specs=in_specs, out_specs=out_specs, check_vma=False
    )
```

```python
import functools
import math

import jax
import jax.numpy as jnp
from jax import lax
from jax.experimental import pallas as pl
from jax.experimental.pallas import tpu as pltpu
from jax.sharding import PartitionSpec as P

T = 128
BATCH = 8
WAYS = 2
BF = jnp.bfloat16
F32 = jnp.float32


def dot(left, right):
    return lax.dot_general(left, right, (((1,), (0,)), ((), ())), preferred_element_type=F32)


def dot_nt(left, right):
    return lax.dot_general(left, right, (((1,), (1,)), ((), ())), preferred_element_type=F32)


def dot_tn(left, right):
    return lax.dot_general(left, right, (((0,), (0,)), ((), ())), preferred_element_type=F32)


def halves(whole):
    upper = whole.astype(BF)
    return upper, (whole - upper.astype(F32)).astype(BF)


def feature(pre):
    slope = jnp.exp(jnp.minimum(pre, 0.0))
    return slope + jnp.maximum(pre, 0.0), slope


def as_columns(row):
    return jnp.broadcast_to(row, (T, T)).T


def marker(rows):
    lane = lax.broadcasted_iota(jnp.int32, (rows, T), 1)
    return jnp.where(lane == 0, 1.0, 0.0).astype(BF)


def inverse(value):
    guess = pl.reciprocal(value, approx=True)
    return guess * (2.0 - value * guess)


def place_rows(target, pieces, axis):
    here = lax.axis_index(axis) if len(pieces) > 1 else jnp.int32(0)
    rows = pieces[0].shape[0]
    for step, piece in enumerate(pieces):
        start = pl.multiple_of((here ^ step) * rows, 16)
        target[pl.ds(start, rows), :] = piece[...].astype(target.dtype)


def attend(*refs, tiles, heads, shares, extra, scale, inv):
    refs = list(refs)

    def take(count):
        taken = refs[:count]
        del refs[:count]
        return taken

    kv_in, q_in = take(tiles), take(tiles)
    past_in, seg_ref, past_seg_ref, seg_scalar, fq_ref, fk_ref = take(6)
    extra_ref = take(1)[0] if extra else None
    err_ref, msg_ref, gkeys_ref, kv, slope_out = take(5)
    share_refs = take(shares)
    past, qs, phis, slopes, dpres, grads, err, sems = refs
    place_rows(kv, kv_in, "ulysses")
    place_rows(past, [past_in.at[d * T : (d + 1) * T] for d in range(tiles)], "ulysses")
    place_rows(qs, q_in, "ulysses")
    length = tiles * T
    group = heads * T

    k_rows, v_rows = kv[:, :T], kv[:, T:]
    kp_rows, vp_rows = past[:, :T], past[:, T:]
    fk = fk_ref[0]
    phi_k, slope_k = feature(dot(k_rows, fk))
    phi_k = phi_k.astype(BF)
    phi_k_t = phi_k.T
    phi_kp, slope_kp = feature(dot(kp_rows, fk))
    first_id = seg_scalar[0, 0].astype(F32)
    seg = seg_ref[...].astype(F32)
    past_seg = past_seg_ref[...].astype(F32)
    past_seg = jnp.where(lax.axis_index("context") > 0, past_seg, -1.0)
    seg_cols = [as_columns(seg[i : i + 1]) for i in range(tiles)]
    past_cols = [as_columns(past_seg[i : i + 1]) for i in range(tiles)]
    past_take = jnp.concatenate([c == first_id for c in past_cols], axis=0)
    phi_kp = jnp.where(past_take, phi_kp, 0.0).astype(BF)
    state = dot_tn(phi_kp, jnp.concatenate([vp_rows, jnp.ones((length, T), BF)], axis=1))
    if extra:
        state = state + extra_ref[...]
    norm = state[:, T:]
    st_both = jnp.concatenate(halves(state[:, :T]), axis=1)
    st_t = jnp.concatenate([state[:, :T].T, norm.T[:16]], axis=0)
    st_t_both = jnp.concatenate(halves(st_t), axis=1)
    ones = jnp.ones((16, length), BF)
    v_t = jnp.concatenate([v_rows.T, ones], axis=0)
    rim_v_t = jnp.concatenate([vp_rows[-T:].T, ones[:, :T]], axis=0)

    for h in range(heads):
        pre = dot_nt(fq_ref[h].T, qs[:, h * T : (h + 1) * T])
        phi, slope = feature(pre)
        phi = phi.astype(BF)
        for i in range(tiles):
            phis[i, :, h * T : (h + 1) * T] = phi[:, i * T : (i + 1) * T]
            slopes[i, :, h * T : (h + 1) * T] = slope[:, i * T : (i + 1) * T]

    s_pos = lax.broadcasted_iota(jnp.int32, (T, T), 0)
    t_pos = lax.broadcasted_iota(jnp.int32, (T, T), 1)
    dpk = [jnp.zeros((T, T), F32)] * tiles
    cot = [jnp.zeros((T, T + 16), F32)]
    copies = []

    def spread(tile):
        return jnp.concatenate([tile] * BATCH, axis=1)

    def by_row(whole, row):
        return (whole.reshape(-1, 8, whole.shape[1]) * row[None]).reshape(whole.shape)

    masks = []
    for i in range(tiles):
        n = (i + 1) * T
        seg_row = seg[i : i + 1]
        same = [seg_cols[j] == seg_row for j in range(i + 1)]
        same[i] = same[i] & (s_pos <= t_pos)
        linked = jnp.concatenate([m.astype(F32).astype(BF) for m in same], axis=0)
        lead = jnp.broadcast_to(seg_row == first_id, (T, T)).astype(F32)
        if i == 0:
            rim_k, rim_cols, near_v = kp_rows[-T:], past_cols[-1], rim_v_t
        else:
            rim_k, rim_cols, near_v = k_rows[n - 2 * T : n - T], seg_cols[i - 1], v_t[:, n - 2 * T : n - T]
        seen = (rim_cols == seg_row) & (s_pos > t_pos)
        off = jnp.concatenate([jnp.where(m, 0.0, -1e30) for m in (seen, same[i])], axis=0)
        near_k = jnp.concatenate([rim_k, k_rows[n - T : n]], axis=0)
        near_v = jnp.concatenate([near_v, v_t[:, n - T : n]], axis=1)
        masks.append((linked, lead, off, near_k, near_v))

    def unit(i, first_head):
        n = (i + 1) * T
        lanes = slice(first_head * T, (first_head + BATCH) * T)
        linked, lead, off, near_k, near_v = masks[i]
        linked, off, lead_low = spread(linked), spread(off), spread(lead.astype(BF))
        phi = phis[i, :, lanes]
        scores = dot(phi_k[:n], phi)
        yield
        scores = scores.astype(BF) * linked
        q_rows = jnp.concatenate(
            [qs[n - T : n, h * T : (h + 1) * T] for h in range(first_head, first_head + BATCH)], axis=0
        )
        logits = dot_nt(near_k, q_rows)
        yield
        logits = logits + off
        top = jnp.max(logits, axis=0, keepdims=True)
        phi_lead = phi * lead_low
        both = dot(v_t[:, :n], scores)
        both = both + dot(st_t_both, jnp.concatenate([phi_lead, phi_lead], axis=0))
        yield
        probs = jnp.exp2((logits - top) * (inv * math.log2(math.e))).astype(BF)
        inv_denom = inverse(both[T : T + 8])
        student = by_row(both[:T], inv_denom)
        soft = dot(near_v, probs)
        yield
        gap = student - by_row(soft[:T], inverse(soft[T : T + 8]))
        up = by_row(gap, 32.0 * inv_denom)
        up_low = up.astype(BF)
        d_scores = dot(v_rows[:n], up_low)
        yield
        d_denom = -jnp.sum(up * student, axis=0, keepdims=True)
        d_scores = (d_scores + d_denom).astype(BF) * linked
        up_lead = up_low * lead_low
        d_denom_lead = d_denom * spread(lead[:1])
        d_phi = dot(phi_k_t[:, :n], d_scores)
        d_phi = d_phi + dot(st_both, jnp.concatenate([up_lead, up_lead], axis=0))
        yield
        gap_low = gap.astype(BF)
        for h in range(BATCH):
            err[n - T : n, (first_head + h) * T : (first_head + h + 1) * T] = gap_low[
                :, h * T : (h + 1) * T
            ].T
        if first_head + BATCH == heads:
            copy = pltpu.make_async_copy(err.at[n - T : n], err_ref.at[n - T : n], sems.at[i])
            copy.start()
            copies.append(copy)
        low_rows = jnp.broadcast_to(d_denom_lead, (16, BATCH * T)).astype(BF)
        back = dot_nt(d_scores, phi)
        cot[0] = cot[0] + dot_nt(phi, jnp.concatenate([up_lead, low_rows], axis=0))
        yield
        for j in range(i + 1):
            dpk[j] = dpk[j] + back[j * T : (j + 1) * T]
        d_phi = d_phi + spread(norm) * d_denom_lead
        d_pre = (d_phi * slopes[i, :, lanes]).astype(BF)
        for h in range(BATCH):
            dpres[first_head + h, :, n - T : n] = d_pre[:, h * T : (h + 1) * T]

    waiting = [unit(i, h) for i in range(tiles) for h in range(0, heads, BATCH)]
    active = []
    while waiting or active:
        if waiting and len(active) < WAYS:
            active.append(waiting.pop(0))
        for step in list(active):
            if next(step, "end") == "end":
                active.remove(step)
    cot = cot[0]

    for h in range(heads):
        grad = dot(dpres[h], qs[:, h * T : (h + 1) * T])
        grads[h * T : (h + 1) * T, :] = (grad.T * scale).astype(BF)

    d_phi_k = jnp.concatenate(dpk, axis=0)
    d_pre_k = (d_phi_k * slope_k).astype(BF)
    cot = jnp.concatenate([cot, jnp.zeros((T, T - 16), F32)], axis=1)
    cot_hi, cot_lo = halves(cot)
    vp_mark = jnp.concatenate([vp_rows, marker(length)], axis=1)
    cross = dot_nt(vp_mark, cot_hi) + dot_nt(vp_mark, cot_lo)
    cross = jnp.where(past_take, cross * slope_kp, 0.0).astype(BF)
    grad = dot_tn(k_rows, d_pre_k) + dot_tn(kp_rows, cross)
    grads[group : group + T, :] = (grad * scale).astype(BF)
    msg_lane = lax.broadcasted_iota(jnp.int32, (T, 2 * T), 1)
    msg_ref[...] = jnp.where(msg_lane == T + 1, first_id, cot_hi.astype(F32)).astype(BF)
    gkeys_ref[...] = dot_nt(d_pre_k, fk)
    slope_out[...] = slope_k
    rows = (heads + 1) * T // shares
    here = lax.axis_index("context") if shares > 1 else jnp.int32(0)
    for step, share in enumerate(share_refs):
        share[...] = grads[pl.ds(pl.multiple_of((here ^ step) * rows, 16), rows), :]
    for copy in copies:
        copy.wait()


def settle(seg_ref, msg_ref, gkeys_ref, kv_ref, slope_ref, fk_ref, out_ref, *, tiles):
    ids = msg_ref[:16, T:].astype(F32)
    next_id = jnp.max(jnp.where(lax.broadcasted_iota(jnp.int32, ids.shape, 1) == 1, ids, -1.0))
    seg = seg_ref[...].astype(F32)
    linked = jnp.concatenate([as_columns(seg[i : i + 1]) == next_id for i in range(tiles)], axis=0)
    v_mark = jnp.concatenate([kv_ref[:, T:], marker(tiles * T)], axis=1)
    back = jnp.where(linked, dot_nt(v_mark, msg_ref[...]) * slope_ref[...], 0.0).astype(BF)
    out_ref[...] = (gkeys_ref[...] + dot_nt(back, fk_ref[0])).astype(BF)


def add_up(*refs):
    *pieces, out_ref = refs
    out_ref[...] = functools.reduce(jnp.add, [p[...].astype(F32) for p in pieces]).astype(BF)


def merge(*refs):
    *pieces, q_ref, k_ref, whole = refs
    place_rows(whole, pieces, "context")
    rows = q_ref.shape[0]
    q_ref[...] = whole[:rows]
    k_ref[...] = whole[rows:]


VMEM = pl.BlockSpec(memory_space=pltpu.VMEM)
SMEM = pl.BlockSpec(memory_space=pltpu.SMEM)
ANY = pl.BlockSpec(memory_space=pl.ANY)


def call(kernel, out_shape, in_specs, args, scratch=(), flops=0, moved=0, out_specs=None, **options):
    return pl.pallas_call(
        functools.partial(kernel, **options),
        grid=(1,),
        out_shape=out_shape,
        in_specs=in_specs,
        out_specs=out_specs or jax.tree.map(lambda _: VMEM, out_shape),
        scratch_shapes=scratch,
        compiler_params=pltpu.CompilerParams(vmem_limit_bytes=48 * 1024 * 1024),
        cost_estimate=pl.CostEstimate(flops=flops, bytes_accessed=moved, transcendentals=0),
    )(*args)


def swap(block, axis, step):
    return lax.ppermute(block, axis, [(i, i ^ step) for i in range(lax.axis_size(axis))])


def shift(block, axis, distance):
    devices = range(lax.axis_size(axis))
    return lax.ppermute(block, axis, [(i - distance, i) for i in devices if i - distance in devices])


def far_state(packed, seg, feat_k):
    count, here = lax.axis_size("context"), lax.axis_index("context")
    tiles, spot = lax.axis_size("ulysses"), lax.axis_index("ulysses")
    ids = jnp.take(seg, spot ^ jnp.arange(tiles), axis=0).reshape(-1)
    first_id, last_id = seg[0, 0], seg[-1, -1]
    phi = feature(dot(packed[:, :T], feat_k[0]))[0].astype(BF)
    phi = jnp.where((ids == last_id)[:, None], phi, jnp.zeros_like(phi))
    local = dot_tn(phi, jnp.concatenate([packed[:, T:], jnp.ones_like(phi)], axis=1))
    states, last_ids = lax.all_gather((local, last_id), "context")
    keep = (last_ids == first_id) & (jnp.arange(count) < here - 1)
    return jnp.sum(jnp.where(keep[:, None, None], states, 0.0), axis=0)


def far_cotangent(cot, kv, slope, seg):
    count, here = lax.axis_size("context"), lax.axis_index("context")
    ids = seg.reshape(-1)
    cot = cot.astype(F32) * jnp.concatenate([jnp.ones((T, T)), marker(T)], axis=1)
    cots, first_ids = lax.all_gather((cot, ids[0]), "context")
    keep = (first_ids == ids[-1]) & (jnp.arange(count) > here + 1)
    total = jnp.sum(jnp.where(keep[:, None, None], cots, 0.0), axis=0)
    v_mark = jnp.concatenate([kv[:, T:], marker(ids.shape[0])], axis=1)
    back = jnp.where((ids == ids[-1])[:, None], dot_nt(v_mark, total.astype(BF)) * slope, 0.0)
    return total, dot_tn(kv[:, :T], back.astype(BF))


def on_device(queries, keys, values, segments, feat_q, feat_k):
    tiles, here = lax.axis_size("ulysses"), lax.axis_index("ulysses")
    count = lax.axis_size("context")
    heads, width, _ = feat_q.shape
    length = segments.shape[0]
    far = count * length // 4 > length
    rows = (heads + 1) * width
    shares = count if count <= 4 and rows % (16 * count) == 0 else 1
    scale = 1.0 / math.sqrt(length * count)
    inv = 1.0 / math.sqrt(width)

    kv = [
        jnp.concatenate(
            [lax.dynamic_slice_in_dim(a, (here ^ step) * width, width, 1) for a in (keys, values)],
            axis=1,
        )
        for step in range(tiles)
    ]
    q = [
        lax.dynamic_slice_in_dim(queries, (here ^ step) * heads * width, heads * width, 1)
        for step in range(tiles)
    ]
    kv, q = lax.optimization_barrier((kv, q))
    kv = kv[:1] + [swap(kv[step], "ulysses", step) for step in range(tiles - 1, 0, -1)][::-1]
    q = q[:1] + [swap(q[step], "ulysses", step) for step in range(1, tiles)]
    seg = segments.reshape(tiles, T)
    packed = jnp.concatenate(kv, axis=0)
    past = shift(packed, "context", 1)
    past_seg = shift(seg, "context", 1)

    args = [*kv, *q, past, seg, past_seg, seg, feat_q, feat_k]
    in_specs = [VMEM] * (2 * tiles + 3) + [SMEM, VMEM, VMEM]
    if far:
        args.append(far_state(packed[:length], seg, feat_k))
        in_specs.append(VMEM)
    error, msg, gkeys, kv_rows, slope_k, *grads = call(
        attend,
        [
            jax.ShapeDtypeStruct((length, heads * width), BF),
            jax.ShapeDtypeStruct((width, 2 * width), BF),
            jax.ShapeDtypeStruct((length, width), F32),
            jax.ShapeDtypeStruct((length, 2 * width), BF),
            jax.ShapeDtypeStruct((length, width), F32),
        ]
        + [jax.ShapeDtypeStruct((rows // shares, width), BF)] * shares,
        in_specs,
        args,
        [
            pltpu.VMEM((length, 2 * width), BF),
            pltpu.VMEM((length, heads * width), BF),
            pltpu.VMEM((tiles, width, heads * T), BF),
            pltpu.VMEM((tiles, width, heads * T), F32),
            pltpu.VMEM((heads, width, length), BF),
            pltpu.VMEM((rows, width), BF),
            pltpu.VMEM((length, heads * width), BF),
            pltpu.SemaphoreType.DMA((tiles,)),
        ],
        out_specs=[ANY] + [VMEM] * (4 + shares),
        flops=4_000_000_000,
        moved=4_000_000,
        tiles=tiles,
        heads=heads,
        shares=shares,
        extra=far,
        scale=scale,
        inv=inv,
    )
    came = shift(msg, "context", -1)
    if far:
        more, grad_more = far_cotangent(msg, kv_rows, slope_k, seg)
        came = (came.astype(F32) + more).astype(BF)
        grad_more = (grad_more * scale).astype(BF)
        grads = [grads[0].at[heads * width :].add(grad_more)]
    if shares > 1:
        got = grads[:1] + [swap(grads[step], "context", step) for step in range(shares - 1, 0, -1)]
        came, *got = lax.optimization_barrier((came, *got))
        total = call(
            add_up, jax.ShapeDtypeStruct((rows // shares, width), BF), [VMEM] * shares, got
        )
        pieces = [swap(total, "context", step) for step in range(shares - 1, 0, -1)]
        pieces = [total] + pieces[::-1]
    else:
        pieces = [lax.psum(grads[0], "context")]
    grad_keys = call(
        settle,
        jax.ShapeDtypeStruct((length, width), BF),
        [VMEM] * 6,
        [seg, came, gkeys, kv_rows, slope_k, feat_k],
        tiles=tiles,
    )
    grad_q, grad_k = call(
        merge,
        [
            jax.ShapeDtypeStruct((heads * width, width), F32),
            jax.ShapeDtypeStruct((width, width), F32),
        ],
        [VMEM] * shares,
        pieces,
        [pltpu.VMEM((rows, width), F32)],
    )
    return (
        error,
        grad_keys,
        grad_q.reshape(heads, width, width),
        grad_k.reshape(1, width, width),
    )


def solution(mesh):
    in_specs = (
        P(("dp", "context", "ulysses"), None),
        P(("dp", "context", "ulysses"), None),
        P(("dp", "context", "ulysses"), None),
        P(("dp", "context")),
        P("ulysses", None, None),
        P("ulysses", None, None),
    )
    out_specs = (
        P(("dp", "context"), "ulysses"),
        P(("dp", "context"), "ulysses"),
        P(("dp", "ulysses"), None, None),
        P(("dp", "ulysses"), None, None),
    )
    return jax.shard_map(
        on_device, mesh=mesh, in_specs=in_specs, out_specs=out_specs, check_vma=False
    )
```

```python
import functools
import math

import jax
import jax.numpy as jnp
from jax import lax
from jax.experimental import pallas as pl
from jax.experimental.pallas import tpu as pltpu
from jax.sharding import PartitionSpec as P

T = 128
BATCH = 8
WAYS = 4
BF = jnp.bfloat16
F32 = jnp.float32


def dot(left, right):
    return lax.dot_general(left, right, (((1,), (0,)), ((), ())), preferred_element_type=F32)


def dot_nt(left, right):
    return lax.dot_general(left, right, (((1,), (1,)), ((), ())), preferred_element_type=F32)


def dot_tn(left, right):
    return lax.dot_general(left, right, (((0,), (0,)), ((), ())), preferred_element_type=F32)


def halves(whole):
    upper = whole.astype(BF)
    return upper, (whole - upper.astype(F32)).astype(BF)


def feature(pre):
    slope = jnp.exp(jnp.minimum(pre, 0.0))
    return slope + jnp.maximum(pre, 0.0), slope


def as_columns(row):
    return jnp.broadcast_to(row, (T, T)).T


def inverse(value):
    guess = pl.reciprocal(value, approx=True)
    return guess * (2.0 - value * guess)


def place_rows(target, pieces, axis, order):
    here = lax.axis_index(axis) if len(pieces) > 1 else jnp.int32(0)
    rows = pieces[0].shape[0]
    for step, piece in zip((0, *order), pieces):
        start = pl.multiple_of((here ^ step) * rows, 16)
        target[pl.ds(start, rows), :] = piece[...].astype(target.dtype)


def attend(*refs, tiles, kv_order, q_order, heads, shares, extra, scale, inv):
    refs = list(refs)

    def take(count):
        taken = refs[:count]
        del refs[:count]
        return taken

    kv_in, q_in = take(tiles), take(tiles)
    past_in, seg_ref, past_seg_ref, seg_scalar, fq_ref, fk_ref = take(6)
    extra_ref = take(1)[0] if extra else None
    err_ref, msg_ref, gkeys_ref, kv, slope_out = take(5)
    share_refs = take(shares)
    past, qs, phis, slopes, dpres, grads, err, sems = refs
    place_rows(kv, kv_in, "ulysses", kv_order)
    place_rows(past, [past_in.at[d * T : (d + 1) * T] for d in range(tiles)], "ulysses", kv_order)
    place_rows(qs, q_in, "ulysses", q_order)
    length = tiles * T
    group = heads * T

    k_rows, v_rows = kv[:, :T], kv[:, T:]
    kp_rows, vp_rows = past[:, :T], past[:, T:]
    fk = fk_ref[0]
    phi_k, slope_k = feature(dot(k_rows, fk))
    phi_k = phi_k.astype(BF)
    phi_k_t = phi_k.T
    phi_kp, slope_kp = feature(dot(kp_rows, fk))
    first_id = seg_scalar[0, 0].astype(F32)
    seg = seg_ref[...].astype(F32)
    past_seg = past_seg_ref[...].astype(F32)
    past_seg = jnp.where(lax.axis_index("context") > 0, past_seg, -1.0)
    seg_cols = [as_columns(seg[i : i + 1]) for i in range(tiles)]
    past_cols = [as_columns(past_seg[i : i + 1]) for i in range(tiles)]
    past_take = jnp.concatenate([c == first_id for c in past_cols], axis=0)
    phi_kp = jnp.where(past_take, phi_kp, 0.0).astype(BF)
    state = dot_tn(phi_kp, jnp.concatenate([vp_rows, jnp.ones((length, T), BF)], axis=1))
    if extra:
        state = state + extra_ref[...]
    norm = state[:, T:]
    st = state[:, :T].astype(BF)
    st_t = jnp.concatenate([state[:, :T].T, norm.T[:16]], axis=0).astype(BF)
    ones = jnp.ones((16, length), BF)
    v_t = jnp.concatenate([v_rows.T, ones], axis=0)
    rim_v_t = jnp.concatenate([vp_rows[-T:].T, ones[:, :T]], axis=0)

    for h in range(heads):
        pre = dot_nt(fq_ref[h].T, qs[:, h * T : (h + 1) * T])
        phi, slope = feature(pre)
        phi = phi.astype(BF)
        for i in range(tiles):
            phis[i, :, h * T : (h + 1) * T] = phi[:, i * T : (i + 1) * T]
            slopes[i, :, h * T : (h + 1) * T] = slope[:, i * T : (i + 1) * T]

    s_pos = lax.broadcasted_iota(jnp.int32, (T, T), 0)
    t_pos = lax.broadcasted_iota(jnp.int32, (T, T), 1)
    dpk = [jnp.zeros((T, T), F32)] * tiles
    cot = [jnp.zeros((T + 16, T), F32)]
    copies = []

    def spread(tile):
        return jnp.concatenate([tile] * BATCH, axis=1)

    def by_row(whole, row):
        return (whole.reshape(-1, 8, whole.shape[1]) * row[None]).reshape(whole.shape)

    masks = []
    for i in range(tiles):
        n = (i + 1) * T
        seg_row = seg[i : i + 1]
        same = [seg_cols[j] == seg_row for j in range(i + 1)]
        same[i] = same[i] & (s_pos <= t_pos)
        linked = jnp.concatenate([m.astype(F32).astype(BF) for m in same], axis=0)
        lead = jnp.broadcast_to(seg_row == first_id, (T, T)).astype(F32)
        if i == 0:
            rim_k, rim_cols, near_v = kp_rows[-T:], past_cols[-1], rim_v_t
        else:
            rim_k, rim_cols, near_v = k_rows[n - 2 * T : n - T], seg_cols[i - 1], v_t[:, n - 2 * T : n - T]
        seen = (rim_cols == seg_row) & (s_pos > t_pos)
        off = jnp.concatenate([jnp.where(m, 0.0, -1e30) for m in (seen, same[i])], axis=0)
        near_k = jnp.concatenate([rim_k, k_rows[n - T : n]], axis=0)
        near_v = jnp.concatenate([near_v, v_t[:, n - T : n]], axis=1)
        masks.append((linked, lead, off, near_k, near_v))

    def unit(i, first_head):
        n = (i + 1) * T
        lanes = slice(first_head * T, (first_head + BATCH) * T)
        linked, lead, off, near_k, near_v = masks[i]
        linked, off, lead_low = spread(linked), spread(off), spread(lead.astype(BF))
        phi = phis[i, :, lanes]
        scores = dot(phi_k[:n], phi)
        yield
        scores = scores.astype(BF) * linked
        q_rows = jnp.concatenate(
            [qs[n - T : n, h * T : (h + 1) * T] for h in range(first_head, first_head + BATCH)], axis=0
        )
        logits = dot_nt(near_k, q_rows)
        yield
        logits = logits + off
        top = jnp.max(logits, axis=0, keepdims=True)
        phi_lead = phi * lead_low
        both = dot(
            jnp.concatenate([v_t[:, :n], st_t], axis=1),
            jnp.concatenate([scores, phi_lead], axis=0),
        )
        yield
        probs = jnp.exp2((logits - top) * (inv * math.log2(math.e))).astype(BF)
        inv_denom = inverse(both[T : T + 8])
        student = by_row(both[:T], inv_denom)
        soft = dot(near_v, probs)
        yield
        gap = student - by_row(soft[:T], inverse(soft[T : T + 8]))
        up = by_row(gap, 32.0 * inv_denom)
        up_low = up.astype(BF)
        d_scores = dot(v_rows[:n], up_low)
        yield
        d_denom = -jnp.sum(up * student, axis=0, keepdims=True)
        d_scores = (d_scores + d_denom).astype(BF) * linked
        up_lead = up_low * lead_low
        d_denom_lead = d_denom * spread(lead[:1])
        d_phi = dot(
            jnp.concatenate([phi_k_t[:, :n], st], axis=1),
            jnp.concatenate([d_scores, up_lead], axis=0),
        )
        yield
        gap_low = gap.astype(BF)
        for h in range(BATCH):
            err[n - T : n, (first_head + h) * T : (first_head + h + 1) * T] = gap_low[
                :, h * T : (h + 1) * T
            ].T
        if first_head + BATCH == heads:
            copy = pltpu.make_async_copy(err.at[n - T : n], err_ref.at[n - T : n], sems.at[i])
            copy.start()
            copies.append(copy)
        low_rows = jnp.broadcast_to(d_denom_lead, (16, BATCH * T)).astype(BF)
        back = dot_nt(d_scores, phi)
        cot[0] = cot[0] + dot_nt(jnp.concatenate([up_lead, low_rows], axis=0), phi)
        yield
        for j in range(i + 1):
            dpk[j] = dpk[j] + back[j * T : (j + 1) * T]
        d_phi = d_phi + spread(norm) * d_denom_lead
        d_pre = (d_phi * slopes[i, :, lanes]).astype(BF)
        for h in range(BATCH):
            dpres[first_head + h, :, n - T : n] = d_pre[:, h * T : (h + 1) * T]

    waiting = [unit(i, h) for i in range(tiles) for h in range(0, heads, BATCH)]
    active = []
    while waiting or active:
        if waiting and len(active) < WAYS:
            active.append(waiting.pop(0))
        for step in list(active):
            if next(step, "end") == "end":
                active.remove(step)
    cot = cot[0]

    for h in range(heads):
        grad = dot(dpres[h], qs[:, h * T : (h + 1) * T])
        grads[h * T : (h + 1) * T, :] = (grad.T * scale).astype(BF)

    d_phi_k = jnp.concatenate(dpk, axis=0)
    d_pre_k = (d_phi_k * slope_k).astype(BF)
    cot_hi, cot_lo = halves(cot)
    cross = dot(vp_rows, cot_hi[:T]) + dot(vp_rows, cot_lo[:T]) + cot[T : T + 1]
    cross = jnp.where(past_take, cross * slope_kp, 0.0).astype(BF)
    grad = dot_tn(k_rows, d_pre_k) + dot_tn(kp_rows, cross)
    grads[group : group + T, :] = (grad * scale).astype(BF)
    row = lax.broadcasted_iota(jnp.int32, cot.shape, 0)
    msg_ref[...] = jnp.where(row > T, first_id, cot).astype(BF)
    gkeys_ref[...] = dot_nt(d_pre_k, fk)
    slope_out[...] = slope_k
    rows = (heads + 1) * T // shares
    here = lax.axis_index("context") if shares > 1 else jnp.int32(0)
    for step, share in enumerate(share_refs):
        share[...] = grads[pl.ds(pl.multiple_of((here ^ step) * rows, 16), rows), :]
    for copy in copies:
        copy.wait()


def settle(seg_ref, msg_ref, gkeys_ref, kv_ref, slope_ref, fk_ref, out_ref, *, tiles):
    norm_row = msg_ref[T:, :].astype(F32)
    next_id = jnp.max(norm_row[1:2])
    seg = seg_ref[...].astype(F32)
    linked = jnp.concatenate([as_columns(seg[i : i + 1]) == next_id for i in range(tiles)], axis=0)
    back = dot(kv_ref[:, T:], msg_ref[:T, :]) + norm_row[:1]
    back = jnp.where(linked, back * slope_ref[...], 0.0).astype(BF)
    out_ref[...] = (gkeys_ref[...] + dot_nt(back, fk_ref[0])).astype(BF)


def add_up(*refs):
    *pieces, out_ref = refs
    out_ref[...] = functools.reduce(jnp.add, [p[...].astype(F32) for p in pieces]).astype(BF)


def merge(*refs, order):
    *pieces, q_ref, k_ref, whole = refs
    place_rows(whole, pieces, "context", order)
    rows = q_ref.shape[0]
    q_ref[...] = whole[:rows]
    k_ref[...] = whole[rows:]


VMEM = pl.BlockSpec(memory_space=pltpu.VMEM)
SMEM = pl.BlockSpec(memory_space=pltpu.SMEM)
ANY = pl.BlockSpec(memory_space=pl.ANY)


def call(kernel, out_shape, in_specs, args, scratch=(), flops=0, moved=0, out_specs=None, **options):
    return pl.pallas_call(
        functools.partial(kernel, **options),
        grid=(1,),
        out_shape=out_shape,
        in_specs=in_specs,
        out_specs=out_specs or jax.tree.map(lambda _: VMEM, out_shape),
        scratch_shapes=scratch,
        compiler_params=pltpu.CompilerParams(vmem_limit_bytes=48 * 1024 * 1024),
        cost_estimate=pl.CostEstimate(flops=flops, bytes_accessed=moved, transcendentals=0),
    )(*args)


def swap(block, axis, step):
    return lax.ppermute(block, axis, [(i, i ^ step) for i in range(lax.axis_size(axis))])


def shift(block, axis, distance, wrap):
    count = lax.axis_size(axis)
    pairs = [(i, (i + distance) % count) for i in range(count) if wrap or 0 <= i + distance < count]
    return lax.ppermute(block, axis, pairs)


def far_state(packed, seg, feat_k):
    count, here = lax.axis_size("context"), lax.axis_index("context")
    tiles, spot = lax.axis_size("ulysses"), lax.axis_index("ulysses")
    ids = jnp.take(seg, spot ^ jnp.arange(tiles), axis=0).reshape(-1)
    first_id, last_id = seg[0, 0], seg[-1, -1]
    phi = feature(dot(packed[:, :T], feat_k[0]))[0].astype(BF)
    phi = jnp.where((ids == last_id)[:, None], phi, jnp.zeros_like(phi))
    local = dot_tn(phi, jnp.concatenate([packed[:, T:], jnp.ones_like(phi)], axis=1))
    states, last_ids = lax.all_gather((local, last_id), "context")
    keep = (last_ids == first_id) & (jnp.arange(count) < here - 1)
    return jnp.sum(jnp.where(keep[:, None, None], states, 0.0), axis=0)


def far_cotangent(cot, kv, slope, seg):
    count, here = lax.axis_size("context"), lax.axis_index("context")
    ids = seg.reshape(-1)
    cot = jnp.where(jnp.arange(T + 16)[:, None] > T, 0.0, cot.astype(F32))
    cots, first_ids = lax.all_gather((cot, ids[0]), "context")
    keep = (first_ids == ids[-1]) & (jnp.arange(count) > here + 1)
    total = jnp.sum(jnp.where(keep[:, None, None], cots, 0.0), axis=0)
    back = (dot(kv[:, T:], total[:T].astype(BF)) + total[T]) * slope
    back = jnp.where((ids == ids[-1])[:, None], back, 0.0)
    return total, dot_tn(kv[:, :T], back.astype(BF))


def on_device(queries, keys, values, segments, feat_q, feat_k):
    tiles, here = lax.axis_size("ulysses"), lax.axis_index("ulysses")
    count = lax.axis_size("context")
    heads, width, _ = feat_q.shape
    length = segments.shape[0]
    far = count * length // 4 > length
    rows = (heads + 1) * width
    shares = count if count <= 4 and rows % (16 * count) == 0 else 1
    scale = 1.0 / math.sqrt(length * count)
    kv_order = q_order = range(1, tiles)
    send_order = range(1, shares)
    share_order = sorted(range(1, shares), key=lambda step: (2, 1, 3).index(step))
    inv = 1.0 / math.sqrt(width)

    kv = [
        jnp.concatenate(
            [lax.dynamic_slice_in_dim(a, (here ^ step) * width, width, 1) for a in (keys, values)],
            axis=1,
        )
        for step in range(tiles)
    ]
    q = [
        lax.dynamic_slice_in_dim(queries, (here ^ step) * heads * width, heads * width, 1)
        for step in range(tiles)
    ]
    kv, q = lax.optimization_barrier((kv, q))
    kv = kv[:1] + [swap(kv[step], "ulysses", step) for step in kv_order]
    q = q[:1] + [swap(q[step], "ulysses", step) for step in q_order]
    seg = segments.reshape(tiles, T)
    packed = jnp.concatenate(kv, axis=0)
    past = shift(packed, "context", 1, True)
    past_seg = shift(seg, "context", 1, True)

    args = [*kv, *q, past, seg, past_seg, seg, feat_q, feat_k]
    in_specs = [VMEM] * (2 * tiles + 3) + [SMEM, VMEM, VMEM]
    if far:
        args.append(far_state(packed[:length], seg, feat_k))
        in_specs.append(VMEM)
    error, msg, gkeys, kv_rows, slope_k, *grads = call(
        attend,
        [
            jax.ShapeDtypeStruct((length, heads * width), BF),
            jax.ShapeDtypeStruct((width + 16, width), BF),
            jax.ShapeDtypeStruct((length, width), F32),
            jax.ShapeDtypeStruct((length, 2 * width), BF),
            jax.ShapeDtypeStruct((length, width), F32),
        ]
        + [jax.ShapeDtypeStruct((rows // shares, width), BF)] * shares,
        in_specs,
        args,
        [
            pltpu.VMEM((length, 2 * width), BF),
            pltpu.VMEM((length, heads * width), BF),
            pltpu.VMEM((tiles, width, heads * T), BF),
            pltpu.VMEM((tiles, width, heads * T), F32),
            pltpu.VMEM((heads, width, length), BF),
            pltpu.VMEM((rows, width), BF),
            pltpu.VMEM((length, heads * width), BF),
            pltpu.SemaphoreType.DMA((tiles,)),
        ],
        out_specs=[ANY] + [VMEM] * (4 + shares),
        flops=4_000_000_000,
        moved=4_000_000,
        tiles=tiles,
        kv_order=kv_order,
        q_order=q_order,
        heads=heads,
        shares=shares,
        extra=far,
        scale=scale,
        inv=inv,
    )
    came = shift(msg, "context", -1, False)
    if far:
        more, grad_more = far_cotangent(msg, kv_rows, slope_k, seg)
        came = (came.astype(F32) + more).astype(BF)
        grad_more = (grad_more * scale).astype(BF)
        grads = [grads[0].at[heads * width :].add(grad_more)]
    if shares > 1:
        got = grads[:1] + [swap(grads[step], "context", step) for step in send_order]
        came, *got = lax.optimization_barrier((came, *got))
        total = call(
            add_up, jax.ShapeDtypeStruct((rows // shares, width), BF), [VMEM] * shares, got
        )
        pieces = [total] + [swap(total, "context", step) for step in share_order]
    else:
        pieces = [lax.psum(grads[0], "context")]
    grad_keys = call(
        settle,
        jax.ShapeDtypeStruct((length, width), BF),
        [VMEM] * 6,
        [seg, came, gkeys, kv_rows, slope_k, feat_k],
        tiles=tiles,
    )
    grad_q, grad_k = call(
        merge,
        [
            jax.ShapeDtypeStruct((heads * width, width), F32),
            jax.ShapeDtypeStruct((width, width), F32),
        ],
        [VMEM] * shares,
        pieces,
        [pltpu.VMEM((rows, width), F32)],
        order=share_order,
    )
    return (
        error,
        grad_keys,
        grad_q.reshape(heads, width, width),
        grad_k.reshape(1, width, width),
    )


def solution(mesh):
    in_specs = (
        P(("dp", "context", "ulysses"), None),
        P(("dp", "context", "ulysses"), None),
        P(("dp", "context", "ulysses"), None),
        P(("dp", "context")),
        P("ulysses", None, None),
        P("ulysses", None, None),
    )
    out_specs = (
        P(("dp", "context"), "ulysses"),
        P(("dp", "context"), "ulysses"),
        P(("dp", "ulysses"), None, None),
        P(("dp", "ulysses"), None, None),
    )
    return jax.shard_map(
        on_device, mesh=mesh, in_specs=in_specs, out_specs=out_specs, check_vma=False
    )
```

```python
import functools
import math

import jax
import jax.numpy as jnp
from jax import lax
from jax.experimental import pallas as pl
from jax.experimental.pallas import tpu as pltpu
from jax.sharding import PartitionSpec as P

T = 128
BATCH = 8
WAYS = 4
BF = jnp.bfloat16
F32 = jnp.float32


def dot(left, right):
    return lax.dot_general(left, right, (((1,), (0,)), ((), ())), preferred_element_type=F32)


def dot_nt(left, right):
    return lax.dot_general(left, right, (((1,), (1,)), ((), ())), preferred_element_type=F32)


def dot_tn(left, right):
    return lax.dot_general(left, right, (((0,), (0,)), ((), ())), preferred_element_type=F32)


def halves(whole):
    upper = whole.astype(BF)
    return upper, (whole - upper.astype(F32)).astype(BF)


def feature(pre):
    slope = jnp.exp(jnp.minimum(pre, 0.0))
    return slope + jnp.maximum(pre, 0.0), slope


def as_columns(row):
    return jnp.broadcast_to(row, (T, T)).T


def inverse(value):
    guess = pl.reciprocal(value, approx=True)
    return guess * (2.0 - value * guess)


def place_rows(target, pieces, axis, order):
    here = lax.axis_index(axis) if len(pieces) > 1 else jnp.int32(0)
    rows = pieces[0].shape[0]
    for step, piece in zip((0, *order), pieces):
        start = pl.multiple_of((here ^ step) * rows, 16)
        target[pl.ds(start, rows), :] = piece[...].astype(target.dtype)


def attend(*refs, tiles, kv_order, q_order, heads, shares, extra, scale, inv):
    refs = list(refs)

    def take(count):
        taken = refs[:count]
        del refs[:count]
        return taken

    kv_in, q_in = take(tiles), take(tiles)
    past_in, seg_ref, past_seg_ref, seg_scalar, fq_ref, fk_ref = take(6)
    extra_ref = take(1)[0] if extra else None
    err_ref, msg_ref, gkeys_ref, kv, slope_out = take(5)
    share_refs = take(shares)
    past, qs, phis, slopes, dpres, grads, err, sems = refs
    place_rows(kv, kv_in, "ulysses", kv_order)
    place_rows(past, [past_in.at[d * T : (d + 1) * T] for d in range(tiles)], "ulysses", kv_order)
    place_rows(qs, q_in, "ulysses", q_order)
    length = tiles * T
    group = heads * T

    k_rows, v_rows = kv[:, :T], kv[:, T:]
    kp_rows, vp_rows = past[:, :T], past[:, T:]
    fk = fk_ref[0]
    phi_k, slope_k = feature(dot(k_rows, fk))
    phi_k = phi_k.astype(BF)
    phi_k_t = phi_k.T
    phi_kp, slope_kp = feature(dot(kp_rows, fk))
    first_id = seg_scalar[0, 0].astype(F32)
    seg = seg_ref[...].astype(F32)
    past_seg = past_seg_ref[...].astype(F32)
    past_seg = jnp.where(lax.axis_index("context") > 0, past_seg, -1.0)
    seg_cols = [as_columns(seg[i : i + 1]) for i in range(tiles)]
    past_cols = [as_columns(past_seg[i : i + 1]) for i in range(tiles)]
    past_take = jnp.concatenate([c == first_id for c in past_cols], axis=0)
    phi_kp = jnp.where(past_take, phi_kp, 0.0).astype(BF)
    state = dot_tn(phi_kp, jnp.concatenate([vp_rows, jnp.ones((length, T), BF)], axis=1))
    if extra:
        state = state + extra_ref[...]
    norm = state[:, T:]
    st = state[:, :T].astype(BF)
    st_t = jnp.concatenate([state[:, :T].T, norm.T[:16]], axis=0).astype(BF)
    ones = jnp.ones((16, length), BF)
    v_t = jnp.concatenate([v_rows.T, ones], axis=0)
    rim_v_t = jnp.concatenate([vp_rows[-T:].T, ones[:, :T]], axis=0)

    for h in range(heads):
        pre = dot_nt(fq_ref[h].T, qs[:, h * T : (h + 1) * T])
        phi, slope = feature(pre)
        phi = phi.astype(BF)
        for i in range(tiles):
            phis[i, :, h * T : (h + 1) * T] = phi[:, i * T : (i + 1) * T]
            slopes[i, :, h * T : (h + 1) * T] = slope[:, i * T : (i + 1) * T]

    s_pos = lax.broadcasted_iota(jnp.int32, (T, T), 0)
    t_pos = lax.broadcasted_iota(jnp.int32, (T, T), 1)
    dpk = [jnp.zeros((T, T), F32)] * tiles
    cot = [jnp.zeros((T + 16, T), F32)]
    copies = []
    eye = (s_pos == t_pos).astype(F32).astype(BF)

    def spread(tile):
        return jnp.concatenate([tile] * BATCH, axis=1)

    def by_row(whole, row):
        return (whole.reshape(-1, 8, whole.shape[1]) * row[None]).reshape(whole.shape)

    masks = []
    for i in range(tiles):
        n = (i + 1) * T
        seg_row = seg[i : i + 1]
        same = [seg_cols[j] == seg_row for j in range(i + 1)]
        same[i] = same[i] & (s_pos <= t_pos)
        linked = jnp.concatenate([m.astype(F32).astype(BF) for m in same], axis=0)
        lead = jnp.broadcast_to(seg_row == first_id, (T, T)).astype(F32)
        if i == 0:
            rim_k, rim_cols, near_v = kp_rows[-T:], past_cols[-1], rim_v_t
        else:
            rim_k, rim_cols, near_v = k_rows[n - 2 * T : n - T], seg_cols[i - 1], v_t[:, n - 2 * T : n - T]
        seen = (rim_cols == seg_row) & (s_pos > t_pos)
        off = jnp.concatenate([jnp.where(m, 0.0, -1e30) for m in (seen, same[i])], axis=0)
        near_k = jnp.concatenate([rim_k, k_rows[n - T : n]], axis=0)
        near_v = jnp.concatenate([near_v, v_t[:, n - T : n]], axis=1)
        masks.append((linked, lead, off, near_k, near_v))

    def unit(i, first_head):
        n = (i + 1) * T
        lanes = slice(first_head * T, (first_head + BATCH) * T)
        linked, lead, off, near_k, near_v = masks[i]
        linked, off, lead_low = spread(linked), spread(off), spread(lead.astype(BF))
        phi = phis[i, :, lanes]
        scores = dot(phi_k[:n], phi)
        yield
        scores = scores.astype(BF) * linked
        q_rows = jnp.concatenate(
            [qs[n - T : n, h * T : (h + 1) * T] for h in range(first_head, first_head + BATCH)], axis=0
        )
        logits = dot_nt(near_k, q_rows)
        yield
        logits = logits + off
        top = jnp.max(logits, axis=0, keepdims=True)
        phi_lead = phi * lead_low
        both = dot(
            jnp.concatenate([v_t[:, :n], st_t], axis=1),
            jnp.concatenate([scores, phi_lead], axis=0),
        )
        yield
        probs = jnp.exp2((logits - top) * (inv * math.log2(math.e))).astype(BF)
        inv_denom = inverse(both[T : T + 8])
        student = by_row(both[:T], inv_denom)
        soft = dot(near_v, probs)
        yield
        gap = student - by_row(soft[:T], inverse(soft[T : T + 8]))
        up = by_row(gap, 32.0 * inv_denom)
        up_low = up.astype(BF)
        d_scores = dot(v_rows[:n], up_low)
        yield
        d_denom = -jnp.sum(up * student, axis=0, keepdims=True)
        d_scores = (d_scores + d_denom).astype(BF) * linked
        up_lead = up_low * lead_low
        d_denom_lead = d_denom * spread(lead[:1])
        d_phi = dot(
            jnp.concatenate([phi_k_t[:, :n], st], axis=1),
            jnp.concatenate([d_scores, up_lead], axis=0),
        )
        yield
        gap_low = gap.astype(BF)
        for h in range(BATCH):
            err[n - T : n, (first_head + h) * T : (first_head + h + 1) * T] = dot_nt(
                eye, gap_low[:, h * T : (h + 1) * T]
            ).astype(BF)
        if first_head + BATCH == heads:
            copy = pltpu.make_async_copy(err.at[n - T : n], err_ref.at[n - T : n], sems.at[i])
            copy.start()
            copies.append(copy)
        low_rows = jnp.broadcast_to(d_denom_lead, (16, BATCH * T)).astype(BF)
        back = dot_nt(d_scores, phi)
        cot[0] = cot[0] + dot_nt(jnp.concatenate([up_lead, low_rows], axis=0), phi)
        yield
        for j in range(i + 1):
            dpk[j] = dpk[j] + back[j * T : (j + 1) * T]
        d_phi = d_phi + spread(norm) * d_denom_lead
        d_pre = (d_phi * slopes[i, :, lanes]).astype(BF)
        for h in range(BATCH):
            dpres[first_head + h, :, n - T : n] = d_pre[:, h * T : (h + 1) * T]

    waiting = [unit(i, h) for i in range(tiles) for h in range(0, heads, BATCH)]
    active = []
    while waiting or active:
        if waiting and len(active) < WAYS:
            active.append(waiting.pop(0))
        for step in list(active):
            if next(step, "end") == "end":
                active.remove(step)
    cot = cot[0]

    d_phi_k = jnp.concatenate(dpk, axis=0)
    d_pre_k = (d_phi_k * slope_k).astype(BF)
    cross = dot(vp_rows, cot[:T].astype(BF)) + cot[T : T + 1]
    cross = jnp.where(past_take, cross * slope_kp, 0.0).astype(BF)
    grad = dot_tn(
        jnp.concatenate([k_rows, kp_rows], axis=0), jnp.concatenate([d_pre_k, cross], axis=0)
    )
    grads[group : group + T, :] = (grad * scale).astype(BF)
    row = lax.broadcasted_iota(jnp.int32, cot.shape, 0)
    msg_ref[...] = jnp.where(row > T, first_id, cot).astype(BF)
    gkeys_ref[...] = dot_nt(d_pre_k, fk)
    slope_out[...] = slope_k
    for h in range(heads):
        grad = dot(dpres[h], qs[:, h * T : (h + 1) * T])
        grads[h * T : (h + 1) * T, :] = (grad.T * scale).astype(BF)

    rows = (heads + 1) * T // shares
    here = lax.axis_index("context") if shares > 1 else jnp.int32(0)
    for step, share in enumerate(share_refs):
        share[...] = grads[pl.ds(pl.multiple_of((here ^ step) * rows, 16), rows), :]
    for copy in copies:
        copy.wait()


def settle(seg_ref, msg_ref, gkeys_ref, kv_ref, slope_ref, fk_ref, out_ref, *, tiles):
    norm_row = msg_ref[T:, :].astype(F32)
    next_id = jnp.max(norm_row[1:2])
    seg = seg_ref[...].astype(F32)
    linked = jnp.concatenate([as_columns(seg[i : i + 1]) == next_id for i in range(tiles)], axis=0)
    back = dot(kv_ref[:, T:], msg_ref[:T, :]) + norm_row[:1]
    back = jnp.where(linked, back * slope_ref[...], 0.0).astype(BF)
    out_ref[...] = (gkeys_ref[...] + dot_nt(back, fk_ref[0])).astype(BF)


def add_up(*refs):
    *pieces, out_ref = refs
    out_ref[...] = functools.reduce(jnp.add, [p[...].astype(F32) for p in pieces]).astype(BF)


def merge(*refs, steps, count):
    pieces, (q_ref, k_ref, wide, sems) = refs[: len(steps)], refs[-4:]
    here = lax.axis_index("context")
    rows = pieces[0].shape[0]
    last = (count - 1) * rows
    split = q_ref.shape[0] - last

    def copies(slot, step):
        owner = here ^ step
        start = pl.multiple_of(jnp.minimum(owner, count - 2) * rows, 16)
        inner = pltpu.make_async_copy(wide.at[slot], q_ref.at[pl.ds(start, rows)], sems.at[slot, 0])
        edge = [
            pltpu.make_async_copy(wide.at[slot, :split], q_ref.at[last:], sems.at[slot, 0]),
            pltpu.make_async_copy(wide.at[slot, split:], k_ref, sems.at[slot, 1]),
        ]
        return owner < count - 1, [inner], edge

    def each(slot, step, action):
        within, inner, edge = copies(slot, step)

        @pl.when(within)
        def _():
            for copy in inner:
                action(copy)

        @pl.when(jnp.logical_not(within))
        def _():
            for copy in edge:
                action(copy)

    for slot, step in enumerate(steps):
        wide[slot] = pieces[slot][...].astype(F32)
        each(slot, step, lambda copy: copy.start())
    for slot, step in enumerate(steps):
        each(slot, step, lambda copy: copy.wait())


VMEM = pl.BlockSpec(memory_space=pltpu.VMEM)
SMEM = pl.BlockSpec(memory_space=pltpu.SMEM)
ANY = pl.BlockSpec(memory_space=pl.ANY)


def call(kernel, out_shape, in_specs, args, scratch=(), flops=0, moved=0, out_specs=None, aliases=None, **options):
    return pl.pallas_call(
        functools.partial(kernel, **options),
        grid=(1,),
        out_shape=out_shape,
        in_specs=in_specs,
        out_specs=out_specs or jax.tree.map(lambda _: VMEM, out_shape),
        scratch_shapes=scratch,
        input_output_aliases=aliases or {},
        compiler_params=pltpu.CompilerParams(vmem_limit_bytes=48 * 1024 * 1024),
        cost_estimate=pl.CostEstimate(flops=flops, bytes_accessed=moved, transcendentals=0),
    )(*args)


def swap(block, axis, step):
    return lax.ppermute(block, axis, [(i, i ^ step) for i in range(lax.axis_size(axis))])


def shift(block, axis, distance, wrap):
    count = lax.axis_size(axis)
    pairs = [(i, (i + distance) % count) for i in range(count) if wrap or 0 <= i + distance < count]
    return lax.ppermute(block, axis, pairs)


def far_state(packed, seg, feat_k):
    count, here = lax.axis_size("context"), lax.axis_index("context")
    tiles, spot = lax.axis_size("ulysses"), lax.axis_index("ulysses")
    ids = jnp.take(seg, spot ^ jnp.arange(tiles), axis=0).reshape(-1)
    first_id, last_id = seg[0, 0], seg[-1, -1]
    phi = feature(dot(packed[:, :T], feat_k[0]))[0].astype(BF)
    phi = jnp.where((ids == last_id)[:, None], phi, jnp.zeros_like(phi))
    local = dot_tn(phi, jnp.concatenate([packed[:, T:], jnp.ones_like(phi)], axis=1))
    states, last_ids = lax.all_gather((local, last_id), "context")
    keep = (last_ids == first_id) & (jnp.arange(count) < here - 1)
    return jnp.sum(jnp.where(keep[:, None, None], states, 0.0), axis=0)


def far_cotangent(cot, kv, slope, seg):
    count, here = lax.axis_size("context"), lax.axis_index("context")
    ids = seg.reshape(-1)
    cot = jnp.where(jnp.arange(T + 16)[:, None] > T, 0.0, cot.astype(F32))
    cots, first_ids = lax.all_gather((cot, ids[0]), "context")
    keep = (first_ids == ids[-1]) & (jnp.arange(count) > here + 1)
    total = jnp.sum(jnp.where(keep[:, None, None], cots, 0.0), axis=0)
    back = (dot(kv[:, T:], total[:T].astype(BF)) + total[T]) * slope
    back = jnp.where((ids == ids[-1])[:, None], back, 0.0)
    return total, dot_tn(kv[:, :T], back.astype(BF))


def on_device(queries, keys, values, segments, feat_q, feat_k):
    tiles, here = lax.axis_size("ulysses"), lax.axis_index("ulysses")
    count = lax.axis_size("context")
    heads, width, _ = feat_q.shape
    length = segments.shape[0]
    far = count * length // 4 > length
    rows = (heads + 1) * width
    shares = count if count <= 4 and rows % (16 * count) == 0 else 1
    scale = 1.0 / math.sqrt(length * count)
    kv_order = q_order = range(1, tiles)
    send_order = range(1, shares)
    share_order = sorted(range(1, shares), key=(2, 1, 3).index)
    inv = 1.0 / math.sqrt(width)

    kv = [
        jnp.concatenate(
            [lax.dynamic_slice_in_dim(a, (here ^ step) * width, width, 1) for a in (keys, values)],
            axis=1,
        )
        for step in range(tiles)
    ]
    q = [
        lax.dynamic_slice_in_dim(queries, (here ^ step) * heads * width, heads * width, 1)
        for step in range(tiles)
    ]
    kv, q = lax.optimization_barrier((kv, q))
    kv = kv[:1] + [swap(kv[step], "ulysses", step) for step in kv_order]
    q = q[:1] + [swap(q[step], "ulysses", step) for step in q_order]
    seg = segments.reshape(tiles, T)
    packed = jnp.concatenate(kv, axis=0)
    past = shift(packed, "context", 1, True)
    past_seg = shift(seg, "context", 1, True)

    args = [*kv, *q, past, seg, past_seg, seg, feat_q, feat_k]
    in_specs = [VMEM] * (2 * tiles + 3) + [SMEM, VMEM, VMEM]
    if far:
        args.append(far_state(packed[:length], seg, feat_k))
        in_specs.append(VMEM)
    error, msg, gkeys, kv_rows, slope_k, *grads = call(
        attend,
        [
            jax.ShapeDtypeStruct((length, heads * width), BF),
            jax.ShapeDtypeStruct((width + 16, width), BF),
            jax.ShapeDtypeStruct((length, width), F32),
            jax.ShapeDtypeStruct((length, 2 * width), BF),
            jax.ShapeDtypeStruct((length, width), F32),
        ]
        + [jax.ShapeDtypeStruct((rows // shares, width), BF)] * shares,
        in_specs,
        args,
        [
            pltpu.VMEM((length, 2 * width), BF),
            pltpu.VMEM((length, heads * width), BF),
            pltpu.VMEM((tiles, width, heads * T), BF),
            pltpu.VMEM((tiles, width, heads * T), F32),
            pltpu.VMEM((heads, width, length), BF),
            pltpu.VMEM((rows, width), BF),
            pltpu.VMEM((length, heads * width), BF),
            pltpu.SemaphoreType.DMA((tiles,)),
        ],
        out_specs=[ANY] + [VMEM] * (4 + shares),
        flops=4_000_000_000,
        moved=4_000_000,
        tiles=tiles,
        kv_order=kv_order,
        q_order=q_order,
        heads=heads,
        shares=shares,
        extra=far,
        scale=scale,
        inv=inv,
    )
    came = shift(msg, "context", -1, False)
    if far:
        more, grad_more = far_cotangent(msg, kv_rows, slope_k, seg)
        came = (came.astype(F32) + more).astype(BF)
        grad_more = (grad_more * scale).astype(BF)
        grads = [grads[0].at[heads * width :].add(grad_more)]
    if shares > 1:
        got = grads[:1] + [swap(grads[step], "context", step) for step in send_order]
        came, *got = lax.optimization_barrier((came, *got))
        total = call(
            add_up, jax.ShapeDtypeStruct((rows // shares, width), BF), [VMEM] * shares, got
        )
        pieces = [swap(total, "context", step) for step in share_order]
        out_shape = [
            jax.ShapeDtypeStruct((heads * width, width), F32),
            jax.ShapeDtypeStruct((width, width), F32),
        ]
        parts = [((0, *share_order[1:]), [total] + pieces[1:]), (share_order[:1], pieces[:1])]
        written = []
        for steps, given in parts:
            written = call(
                merge,
                out_shape,
                [VMEM] * len(given) + [ANY] * len(written),
                [*given, *written],
                [
                    pltpu.VMEM((len(given), rows // shares, width), F32),
                    pltpu.SemaphoreType.DMA((len(given), 2)),
                ],
                out_specs=[ANY] * 2,
                aliases={len(given): 0, len(given) + 1: 1} if written else {},
                steps=tuple(steps),
                count=shares,
            )
        grad_q, grad_k = written
    else:
        whole = lax.psum(grads[0], "context").astype(F32)
        grad_q, grad_k = whole[: heads * width], whole[heads * width :]
    grad_keys = call(
        settle,
        jax.ShapeDtypeStruct((length, width), BF),
        [VMEM] * 6,
        [seg, came, gkeys, kv_rows, slope_k, feat_k],
        tiles=tiles,
    )
    return (
        error,
        grad_keys,
        grad_q.reshape(heads, width, width),
        grad_k.reshape(1, width, width),
    )


def solution(mesh):
    in_specs = (
        P(("dp", "context", "ulysses"), None),
        P(("dp", "context", "ulysses"), None),
        P(("dp", "context", "ulysses"), None),
        P(("dp", "context")),
        P("ulysses", None, None),
        P("ulysses", None, None),
    )
    out_specs = (
        P(("dp", "context"), "ulysses"),
        P(("dp", "context"), "ulysses"),
        P(("dp", "ulysses"), None, None),
        P(("dp", "ulysses"), None, None),
    )
    return jax.shard_map(
        on_device, mesh=mesh, in_specs=in_specs, out_specs=out_specs, check_vma=False
    )
```

```python
import functools
import math

import jax
import jax.numpy as jnp
from jax import lax
from jax.experimental import pallas as pl
from jax.experimental.pallas import tpu as pltpu
from jax.sharding import PartitionSpec as P

T = 128
BATCH = 8
WAYS = 4
BF = jnp.bfloat16
F32 = jnp.float32


def dot(left, right):
    return lax.dot_general(left, right, (((1,), (0,)), ((), ())), preferred_element_type=F32)


def dot_nt(left, right):
    return lax.dot_general(left, right, (((1,), (1,)), ((), ())), preferred_element_type=F32)


def dot_tn(left, right):
    return lax.dot_general(left, right, (((0,), (0,)), ((), ())), preferred_element_type=F32)


def halves(whole):
    upper = whole.astype(BF)
    return upper, (whole - upper.astype(F32)).astype(BF)


def feature(pre):
    slope = jnp.exp(jnp.minimum(pre, 0.0))
    return slope + jnp.maximum(pre, 0.0), slope


def as_columns(row):
    return jnp.broadcast_to(row, (T, T)).T


def inverse(value):
    guess = pl.reciprocal(value, approx=True)
    return guess * (2.0 - value * guess)


def place_rows(target, pieces, axis, order):
    here = lax.axis_index(axis) if len(pieces) > 1 else jnp.int32(0)
    rows = pieces[0].shape[0]
    for step, piece in zip((0, *order), pieces):
        start = pl.multiple_of((here ^ step) * rows, 16)
        target[pl.ds(start, rows), :] = piece[...].astype(target.dtype)


def attend(*refs, tiles, kv_order, q_order, heads, shares, extra, scale, inv):
    refs = list(refs)

    def take(count):
        taken = refs[:count]
        del refs[:count]
        return taken

    kv_in, q_in = take(tiles), take(tiles)
    past_in, seg_ref, past_seg_ref, seg_scalar, fq_ref, fk_ref = take(6)
    extra_ref = take(1)[0] if extra else None
    err_ref, msg_ref, gkeys_ref, kv, slope_out = take(5)
    share_refs = take(shares)
    past, qs, phis, slopes, dpres, grads, err, sems = refs
    place_rows(kv, kv_in, "ulysses", kv_order)
    place_rows(past, [past_in.at[d * T : (d + 1) * T] for d in range(tiles)], "ulysses", kv_order)
    place_rows(qs, q_in, "ulysses", q_order)
    length = tiles * T
    group = heads * T

    k_rows, v_rows = kv[:, :T], kv[:, T:]
    kp_rows, vp_rows = past[:, :T], past[:, T:]
    fk = fk_ref[0]
    phi_k, slope_k = feature(dot(k_rows, fk))
    phi_k = phi_k.astype(BF)
    phi_k_t = phi_k.T
    phi_kp, slope_kp = feature(dot(kp_rows, fk))
    first_id = seg_scalar[0, 0].astype(F32)
    seg = seg_ref[...].astype(F32)
    past_seg = past_seg_ref[...].astype(F32)
    past_seg = jnp.where(lax.axis_index("context") > 0, past_seg, -1.0)
    seg_cols = [as_columns(seg[i : i + 1]) for i in range(tiles)]
    past_cols = [as_columns(past_seg[i : i + 1]) for i in range(tiles)]
    past_take = jnp.concatenate([c == first_id for c in past_cols], axis=0)
    phi_kp = jnp.where(past_take, phi_kp, 0.0).astype(BF)
    state = dot_tn(phi_kp, jnp.concatenate([vp_rows, jnp.ones((length, T), BF)], axis=1))
    if extra:
        state = state + extra_ref[...]
    norm = state[:, T:]
    st = state[:, :T].astype(BF)
    st_t = jnp.concatenate([state[:, :T].T, norm.T[:16]], axis=0).astype(BF)
    ones = jnp.ones((16, length), BF)
    v_t = jnp.concatenate([v_rows.T, ones], axis=0)
    rim_v_t = jnp.concatenate([vp_rows[-T:].T, ones[:, :T]], axis=0)

    for h in range(heads):
        pre = dot_nt(fq_ref[h].T, qs[:, h * T : (h + 1) * T])
        phi, slope = feature(pre)
        phi = phi.astype(BF)
        for i in range(tiles):
            phis[i, :, h * T : (h + 1) * T] = phi[:, i * T : (i + 1) * T]
            slopes[i, :, h * T : (h + 1) * T] = slope[:, i * T : (i + 1) * T].astype(BF)

    s_pos = lax.broadcasted_iota(jnp.int32, (T, T), 0)
    t_pos = lax.broadcasted_iota(jnp.int32, (T, T), 1)
    dpk = [jnp.zeros((T, T), F32)] * tiles
    cot = [jnp.zeros((T + 16, T), F32)]
    copies = []
    eye = (s_pos == t_pos).astype(F32).astype(BF)

    def spread(tile):
        return jnp.concatenate([tile] * BATCH, axis=1)

    def by_row(whole, row):
        return (whole.reshape(-1, 8, whole.shape[1]) * row[None]).reshape(whole.shape)

    masks = []
    for i in range(tiles):
        n = (i + 1) * T
        seg_row = seg[i : i + 1]
        same = [seg_cols[j] == seg_row for j in range(i + 1)]
        same[i] = same[i] & (s_pos <= t_pos)
        linked = jnp.concatenate([m.astype(F32).astype(BF) for m in same], axis=0)
        lead = jnp.broadcast_to(seg_row == first_id, (T, T)).astype(F32)
        if i == 0:
            rim_k, rim_cols, near_v = kp_rows[-T:], past_cols[-1], rim_v_t
        else:
            rim_k, rim_cols, near_v = k_rows[n - 2 * T : n - T], seg_cols[i - 1], v_t[:, n - 2 * T : n - T]
        seen = (rim_cols == seg_row) & (s_pos > t_pos)
        off = jnp.concatenate([jnp.where(m, 0.0, -1e30) for m in (seen, same[i])], axis=0)
        near_k = jnp.concatenate([rim_k, k_rows[n - T : n]], axis=0)
        near_v = jnp.concatenate([near_v, v_t[:, n - T : n]], axis=1)
        masks.append((linked, lead, off, near_k, near_v))

    def unit(i, first_head):
        n = (i + 1) * T
        lanes = slice(first_head * T, (first_head + BATCH) * T)
        linked, lead, off, near_k, near_v = masks[i]
        linked, off, lead_low = spread(linked), spread(off), spread(lead.astype(BF))
        phi = phis[i, :, lanes]
        scores = dot(phi_k[:n], phi)
        yield
        scores = scores.astype(BF) * linked
        q_rows = jnp.concatenate(
            [qs[n - T : n, h * T : (h + 1) * T] for h in range(first_head, first_head + BATCH)], axis=0
        )
        logits = dot_nt(near_k, q_rows)
        yield
        logits = logits + off
        top = jnp.max(logits, axis=0, keepdims=True)
        phi_lead = phi * lead_low
        both = dot(
            jnp.concatenate([v_t[:, :n], st_t], axis=1),
            jnp.concatenate([scores, phi_lead], axis=0),
        )
        yield
        probs = jnp.exp2((logits - top) * (inv * math.log2(math.e))).astype(BF)
        inv_denom = inverse(both[T : T + 8])
        student = by_row(both[:T], inv_denom)
        soft = dot(near_v, probs)
        yield
        gap = student - by_row(soft[:T], inverse(soft[T : T + 8]))
        up = by_row(gap, 32.0 * inv_denom)
        up_low = up.astype(BF)
        d_scores = dot(v_rows[:n], up_low)
        yield
        d_denom = -jnp.sum(up * student, axis=0, keepdims=True)
        d_scores = (d_scores + d_denom).astype(BF) * linked
        up_lead = up_low * lead_low
        d_denom_lead = d_denom * spread(lead[:1])
        d_phi = dot(
            jnp.concatenate([phi_k_t[:, :n], st], axis=1),
            jnp.concatenate([d_scores, up_lead], axis=0),
        )
        yield
        gap_low = gap.astype(BF)
        for h in range(BATCH):
            err[n - T : n, (first_head + h) * T : (first_head + h + 1) * T] = dot_nt(
                eye, gap_low[:, h * T : (h + 1) * T]
            ).astype(BF)
        if first_head + BATCH == heads:
            copy = pltpu.make_async_copy(err.at[n - T : n], err_ref.at[n - T : n], sems.at[i])
            copy.start()
            copies.append(copy)
        low_rows = jnp.broadcast_to(d_denom_lead, (16, BATCH * T)).astype(BF)
        back = dot_nt(d_scores, phi)
        cot[0] = cot[0] + dot_nt(jnp.concatenate([up_lead, low_rows], axis=0), phi)
        yield
        for j in range(i + 1):
            dpk[j] = dpk[j] + back[j * T : (j + 1) * T]
        d_phi = d_phi + spread(norm) * d_denom_lead
        d_pre = (d_phi * slopes[i, :, lanes].astype(F32)).astype(BF)
        for h in range(BATCH):
            dpres[first_head + h, :, n - T : n] = d_pre[:, h * T : (h + 1) * T]

    waiting = [unit(i, h) for i in range(tiles) for h in range(0, heads, BATCH)]
    active = []
    while waiting or active:
        if waiting and len(active) < WAYS:
            active.append(waiting.pop(0))
        for step in list(active):
            if next(step, "end") == "end":
                active.remove(step)
    cot = cot[0]

    d_phi_k = jnp.concatenate(dpk, axis=0)
    d_pre_k = (d_phi_k * slope_k).astype(BF)
    cross = dot(vp_rows, cot[:T].astype(BF)) + cot[T : T + 1]
    cross = jnp.where(past_take, cross * slope_kp, 0.0).astype(BF)
    grad = dot_tn(
        jnp.concatenate([k_rows, kp_rows], axis=0), jnp.concatenate([d_pre_k, cross], axis=0)
    )
    grads[group : group + T, :] = (grad * scale).astype(BF)
    row = lax.broadcasted_iota(jnp.int32, cot.shape, 0)
    msg_ref[...] = jnp.where(row > T, first_id, cot).astype(BF)
    gkeys_ref[...] = dot_nt(d_pre_k, fk)
    slope_out[...] = slope_k
    for h in range(heads):
        grad = dot(dpres[h], qs[:, h * T : (h + 1) * T])
        grads[h * T : (h + 1) * T, :] = (grad.T * scale).astype(BF)

    rows = (heads + 1) * T // shares
    here = lax.axis_index("context") if shares > 1 else jnp.int32(0)
    for step, share in enumerate(share_refs):
        share[...] = grads[pl.ds(pl.multiple_of((here ^ step) * rows, 16), rows), :]
    for copy in copies:
        copy.wait()


def settle(seg_ref, msg_ref, gkeys_ref, kv_ref, slope_ref, fk_ref, out_ref, *, tiles):
    norm_row = msg_ref[T:, :].astype(F32)
    next_id = jnp.max(norm_row[1:2])
    seg = seg_ref[...].astype(F32)
    linked = jnp.concatenate([as_columns(seg[i : i + 1]) == next_id for i in range(tiles)], axis=0)
    back = dot(kv_ref[:, T:], msg_ref[:T, :]) + norm_row[:1]
    back = jnp.where(linked, back * slope_ref[...], 0.0).astype(BF)
    out_ref[...] = (gkeys_ref[...] + dot_nt(back, fk_ref[0])).astype(BF)


def add_up(*refs):
    *pieces, out_ref = refs
    out_ref[...] = functools.reduce(jnp.add, [p[...].astype(F32) for p in pieces]).astype(BF)


def merge(*refs, steps, count):
    pieces, (q_ref, k_ref, wide, sems) = refs[: len(steps)], refs[-4:]
    here = lax.axis_index("context")
    rows = pieces[0].shape[0]
    last = (count - 1) * rows
    split = q_ref.shape[0] - last

    def copies(slot, step):
        owner = here ^ step
        start = pl.multiple_of(jnp.minimum(owner, count - 2) * rows, 16)
        inner = pltpu.make_async_copy(wide.at[slot], q_ref.at[pl.ds(start, rows)], sems.at[slot, 0])
        edge = [
            pltpu.make_async_copy(wide.at[slot, :split], q_ref.at[last:], sems.at[slot, 0]),
            pltpu.make_async_copy(wide.at[slot, split:], k_ref, sems.at[slot, 1]),
        ]
        return owner < count - 1, [inner], edge

    def each(slot, step, action):
        within, inner, edge = copies(slot, step)

        @pl.when(within)
        def _():
            for copy in inner:
                action(copy)

        @pl.when(jnp.logical_not(within))
        def _():
            for copy in edge:
                action(copy)

    for slot, step in enumerate(steps):
        wide[slot] = pieces[slot][...].astype(F32)
        each(slot, step, lambda copy: copy.start())
    for slot, step in enumerate(steps):
        each(slot, step, lambda copy: copy.wait())


VMEM = pl.BlockSpec(memory_space=pltpu.VMEM)
SMEM = pl.BlockSpec(memory_space=pltpu.SMEM)
ANY = pl.BlockSpec(memory_space=pl.ANY)


def call(kernel, out_shape, in_specs, args, scratch=(), flops=0, moved=0, out_specs=None, aliases=None, **options):
    return pl.pallas_call(
        functools.partial(kernel, **options),
        grid=(1,),
        out_shape=out_shape,
        in_specs=in_specs,
        out_specs=out_specs or jax.tree.map(lambda _: VMEM, out_shape),
        scratch_shapes=scratch,
        input_output_aliases=aliases or {},
        compiler_params=pltpu.CompilerParams(vmem_limit_bytes=48 * 1024 * 1024),
        cost_estimate=pl.CostEstimate(flops=flops, bytes_accessed=moved, transcendentals=0),
    )(*args)


def swap(block, axis, step):
    return lax.ppermute(block, axis, [(i, i ^ step) for i in range(lax.axis_size(axis))])


def shift(block, axis, distance, wrap):
    count = lax.axis_size(axis)
    pairs = [(i, (i + distance) % count) for i in range(count) if wrap or 0 <= i + distance < count]
    return lax.ppermute(block, axis, pairs)


def far_state(packed, seg, feat_k):
    count, here = lax.axis_size("context"), lax.axis_index("context")
    tiles, spot = lax.axis_size("ulysses"), lax.axis_index("ulysses")
    ids = jnp.take(seg, spot ^ jnp.arange(tiles), axis=0).reshape(-1)
    first_id, last_id = seg[0, 0], seg[-1, -1]
    phi = feature(dot(packed[:, :T], feat_k[0]))[0].astype(BF)
    phi = jnp.where((ids == last_id)[:, None], phi, jnp.zeros_like(phi))
    local = dot_tn(phi, jnp.concatenate([packed[:, T:], jnp.ones_like(phi)], axis=1))
    states, last_ids = lax.all_gather((local, last_id), "context")
    keep = (last_ids == first_id) & (jnp.arange(count) < here - 1)
    return jnp.sum(jnp.where(keep[:, None, None], states, 0.0), axis=0)


def far_cotangent(cot, kv, slope, seg):
    count, here = lax.axis_size("context"), lax.axis_index("context")
    ids = seg.reshape(-1)
    cot = jnp.where(jnp.arange(T + 16)[:, None] > T, 0.0, cot.astype(F32))
    cots, first_ids = lax.all_gather((cot, ids[0]), "context")
    keep = (first_ids == ids[-1]) & (jnp.arange(count) > here + 1)
    total = jnp.sum(jnp.where(keep[:, None, None], cots, 0.0), axis=0)
    back = (dot(kv[:, T:], total[:T].astype(BF)) + total[T]) * slope
    back = jnp.where((ids == ids[-1])[:, None], back, 0.0)
    return total, dot_tn(kv[:, :T], back.astype(BF))


def on_device(queries, keys, values, segments, feat_q, feat_k):
    tiles, here = lax.axis_size("ulysses"), lax.axis_index("ulysses")
    count = lax.axis_size("context")
    heads, width, _ = feat_q.shape
    length = segments.shape[0]
    far = count * length // 4 > length
    rows = (heads + 1) * width
    shares = count if count <= 4 and rows % (16 * count) == 0 else 1
    scale = 1.0 / math.sqrt(length * count)
    kv_order = q_order = range(1, tiles)
    send_order = range(1, shares)
    share_order = sorted(range(1, shares), key=(2, 1, 3).index)
    inv = 1.0 / math.sqrt(width)

    kv = [
        jnp.concatenate(
            [lax.dynamic_slice_in_dim(a, (here ^ step) * width, width, 1) for a in (keys, values)],
            axis=1,
        )
        for step in range(tiles)
    ]
    q = [
        lax.dynamic_slice_in_dim(queries, (here ^ step) * heads * width, heads * width, 1)
        for step in range(tiles)
    ]
    kv, q = lax.optimization_barrier((kv, q))
    kv = kv[:1] + [swap(kv[step], "ulysses", step) for step in kv_order]
    q = q[:1] + [swap(q[step], "ulysses", step) for step in q_order]
    seg = segments.reshape(tiles, T)
    packed = jnp.concatenate(kv, axis=0)
    past = shift(packed, "context", 1, True)
    past_seg = shift(seg, "context", 1, True)

    args = [*kv, *q, past, seg, past_seg, seg, feat_q, feat_k]
    in_specs = [VMEM] * (2 * tiles + 3) + [SMEM, VMEM, VMEM]
    if far:
        args.append(far_state(packed[:length], seg, feat_k))
        in_specs.append(VMEM)
    error, msg, gkeys, kv_rows, slope_k, *grads = call(
        attend,
        [
            jax.ShapeDtypeStruct((length, heads * width), BF),
            jax.ShapeDtypeStruct((width + 16, width), BF),
            jax.ShapeDtypeStruct((length, width), F32),
            jax.ShapeDtypeStruct((length, 2 * width), BF),
            jax.ShapeDtypeStruct((length, width), F32),
        ]
        + [jax.ShapeDtypeStruct((rows // shares, width), BF)] * shares,
        in_specs,
        args,
        [
            pltpu.VMEM((length, 2 * width), BF),
            pltpu.VMEM((length, heads * width), BF),
            pltpu.VMEM((tiles, width, heads * T), BF),
            pltpu.VMEM((tiles, width, heads * T), BF),
            pltpu.VMEM((heads, width, length), BF),
            pltpu.VMEM((rows, width), BF),
            pltpu.VMEM((length, heads * width), BF),
            pltpu.SemaphoreType.DMA((tiles,)),
        ],
        out_specs=[ANY] + [VMEM] * (4 + shares),
        flops=4_000_000_000,
        moved=4_000_000,
        tiles=tiles,
        kv_order=kv_order,
        q_order=q_order,
        heads=heads,
        shares=shares,
        extra=far,
        scale=scale,
        inv=inv,
    )
    came = shift(msg, "context", -1, False)
    if far:
        more, grad_more = far_cotangent(msg, kv_rows, slope_k, seg)
        came = (came.astype(F32) + more).astype(BF)
        grad_more = (grad_more * scale).astype(BF)
        grads = [grads[0].at[heads * width :].add(grad_more)]
    if shares > 1:
        got = grads[:1] + [swap(grads[step], "context", step) for step in send_order]
        came, *got = lax.optimization_barrier((came, *got))
        total = call(
            add_up, jax.ShapeDtypeStruct((rows // shares, width), BF), [VMEM] * shares, got
        )
        pieces = [swap(total, "context", step) for step in share_order]
        out_shape = [
            jax.ShapeDtypeStruct((heads * width, width), F32),
            jax.ShapeDtypeStruct((width, width), F32),
        ]
        parts = [((0, *share_order[1:]), [total] + pieces[1:]), (share_order[:1], pieces[:1])]
        written = []
        for steps, given in parts:
            written = call(
                merge,
                out_shape,
                [VMEM] * len(given) + [ANY] * len(written),
                [*given, *written],
                [
                    pltpu.VMEM((len(given), rows // shares, width), F32),
                    pltpu.SemaphoreType.DMA((len(given), 2)),
                ],
                out_specs=[ANY] * 2,
                aliases={len(given): 0, len(given) + 1: 1} if written else {},
                steps=tuple(steps),
                count=shares,
            )
        grad_q, grad_k = written
    else:
        whole = lax.psum(grads[0], "context").astype(F32)
        grad_q, grad_k = whole[: heads * width], whole[heads * width :]
    grad_keys = call(
        settle,
        jax.ShapeDtypeStruct((length, width), BF),
        [VMEM] * 6,
        [seg, came, gkeys, kv_rows, slope_k, feat_k],
        tiles=tiles,
    )
    return (
        error,
        grad_keys,
        grad_q.reshape(heads, width, width),
        grad_k.reshape(1, width, width),
    )


def solution(mesh):
    in_specs = (
        P(("dp", "context", "ulysses"), None),
        P(("dp", "context", "ulysses"), None),
        P(("dp", "context", "ulysses"), None),
        P(("dp", "context")),
        P("ulysses", None, None),
        P("ulysses", None, None),
    )
    out_specs = (
        P(("dp", "context"), "ulysses"),
        P(("dp", "context"), "ulysses"),
        P(("dp", "ulysses"), None, None),
        P(("dp", "ulysses"), None, None),
    )
    return jax.shard_map(
        on_device, mesh=mesh, in_specs=in_specs, out_specs=out_specs, check_vma=False
    )
```
